256 devices in a mesh: dp: 32 (over z, y), slab: 8 (over x, core).
Axes of the slice: x: 4, y: 4, z: 8, core: 2. Of those that a mesh axis runs over, the one named last changes fastest.
Arguments:
- volume: bfloat16 [256, 16, 8, 128], P('dp', 'slab'), may hold values from -13 to 13, as said below
- flux_target: bfloat16 [256, 3, 8, 4, 64], P('dp', None, 'slab'), may hold values from -6 to 6
- tensor_target: bfloat16 [256, 6], P('dp'), may hold values from -6 to 6
- dest: int32 [256], P('dp'), may hold values from -1 to 255, as said below
- first_weight: bfloat16 [16, 1, 3, 3, 3], replicated, may hold values from -1.25 to 1.25
- first_bias: float32 [16], replicated, may hold values from -3 to 3
- second_weight: bfloat16 [32, 16, 3, 3, 3], replicated, may hold values from -0.3125 to 0.3125
- second_bias: float32 [32], replicated, may hold values from -3 to 3
- short_weight: bfloat16 [32, 16], replicated, may hold values from -1.5 to 1.5
- flux_weight: bfloat16 [3, 32], replicated, may hold values from -1 to 1
- flux_bias: float32 [3], replicated, may hold values from -3 to 3
- tensor_weight: bfloat16 [6, 32], replicated, may hold values from -1 to 1
- tensor_bias: float32 [6], replicated, may hold values from -3 to 3
Outputs:
- flux_pred: bfloat16 [256, 3, 8, 4, 64], P('dp', None, 'slab')
- tensor_pred: bfloat16 [256, 6], P('dp')
- grad_first: float32 [16, 1, 3, 3, 3], replicated
- grad_first_bias: float32 [16], replicated
- grad_second: float32 [32, 16, 3, 3, 3], replicated
- grad_second_bias: float32 [32], replicated
- grad_short: float32 [32, 16], replicated
- grad_flux: float32 [3, 32], replicated
- grad_flux_bias: float32 [3], replicated
- grad_tensor: float32 [6, 32], replicated
- grad_tensor_bias: float32 [6], replicated
The draws below stay inside these ranges and needn't reach their ends.
Inputs may be any that keep to these rules, and one draw needn't show every extreme that they name: `volume`: values are drawn independently per record and z plane; records are fully formed in every slot. `dest`: each entry is -1 (an empty archive slot) or g * 8 + s, sending that record to slot s of trainer group g; no trainer slot is named twice. At most 2 records of one owner go to one trainer group, and some owner sends exactly 2 to some group; some trainer group has all 8 slots filled.
All inputs are finite; a program needn't handle non-finite values.
Results may differ from the reference program's by a relative error of at most 0.0043.
The reference program's roundings to bfloat16 on the way count: a program that leaves them out, or rounds other values in their place, can miss the bound.
Values may be sent and summed in bfloat16 or wider, within the bound.
No kernel may reach another device: no remote copies, remote signals or barrier semaphores. Data moves between devices by JAX's collectives and lax.ppermute only.
A program may use at most 128 MiB of HBM per device.

```python
import jax
import jax.numpy as jnp
from jax import lax

C1 = 16
C2 = 32
NF = 3
NK = 6
XW = 128
YW = 8
R = 8
CAP = 2
RECORDS = 256
Z = 16
ZH = 8
YH = 4
XH = 64
N_DP = 32


def draw_volume(key, part):
    key = jax.random.fold_in(key, 5)
    level_key, value_key = jax.random.split(key)
    levels = jax.random.uniform(level_key, (RECORDS, Z, 1, 1), jnp.float32)
    scales = jnp.exp(2.302585 * (levels - 0.5))
    values = jax.random.truncated_normal(value_key, -4.0, 4.0, (RECORDS, Z, YW, XW), jnp.float32)
    return (values * scales).astype(jnp.bfloat16)


def draw_dest(key, part):
    key = jax.random.fold_in(key, 11)
    keys = jax.random.split(key, 6)
    groups = N_DP
    lowest = max(1, R * 3 // 4)
    loads = jax.random.randint(keys[0], (groups,), lowest, R + 1)
    fullest = jax.random.randint(keys[2], (), 0, groups)
    loads = jnp.where(jnp.arange(groups) == fullest, R, loads)
    order = jax.random.permutation(keys[3], groups)
    order = (order + (groups // 2 - order[0])) % groups
    offsets = order[:R // CAP]
    owners = jnp.arange(groups)[:, None]
    places = jnp.arange(R)[None, :]
    trainers = (owners - offsets[places // CAP]) % groups
    alive = places < loads[trainers]
    slot_orders = jax.vmap(lambda sub: jax.random.permutation(sub, R))(jax.random.split(keys[4], groups))
    slots = slot_orders[trainers, jnp.broadcast_to(places, trainers.shape)]
    values = jnp.where(alive, trainers * R + slots, -1)
    owner_orders = jax.vmap(lambda sub: jax.random.permutation(sub, R))(jax.random.split(keys[5], groups))
    shuffled = jnp.take_along_axis(values, owner_orders, axis=1)
    return shuffled.reshape(RECORDS).astype(jnp.int32)


def shard_levels(rng, extent, cuts, least, high):
    level, own = 1.0, jax.random.fold_in(rng, 6)
    for position, parts in cuts:
        draws = jnp.exp(jax.random.uniform(jax.random.fold_in(own, position), (parts,), jnp.float32, least / len(cuts), high / len(cuts)))
        level = level * jnp.repeat(draws, extent[position] // parts).reshape([-1 if axis == position else 1 for axis in range(len(extent))])
    return level


def gaussian(key, extent, spread, limit, cuts=(), kind=jnp.bfloat16):
    loudness = shard_levels(key, extent, cuts, -0.22, 0.18) if cuts else 1.0
    entries = jax.random.normal(key, extent, jnp.float32) * spread * loudness
    return jnp.minimum(jnp.maximum(entries, -limit), limit).astype(kind)


def setup_inputs(seed: int = 0) -> dict:
    seeds = jax.random.split(jax.random.key(seed), 14)
    return {
        "volume": draw_volume(jax.random.fold_in(seeds[13], 71), 0),
        "flux_target": gaussian(seeds[1], (RECORDS, NF, ZH, YH, XH), 1.0, 6.0, ((0, 32), (2, 8))),
        "tensor_target": gaussian(seeds[2], (RECORDS, NK), 1.0, 6.0, ((0, 32),)),
        "dest": draw_dest(jax.random.fold_in(seeds[13], 71), 0),
        "first_weight": gaussian(seeds[4], (C1, 1, 3, 3, 3), 27 ** -0.5, 1.25),
        "first_bias": gaussian(seeds[5], (C1,), 0.3, 3.0, (), jnp.float32),
        "second_weight": gaussian(seeds[6], (C2, C1, 3, 3, 3), (27 * C1) ** -0.5, 0.3125),
        "second_bias": gaussian(seeds[7], (C2,), 0.3, 3.0, (), jnp.float32),
        "short_weight": gaussian(seeds[8], (C2, C1), C1 ** -0.5, 1.5),
        "flux_weight": gaussian(seeds[9], (NF, C2), C2 ** -0.5, 1.0),
        "flux_bias": gaussian(seeds[10], (NF,), 0.5, 3.0, (), jnp.float32),
        "tensor_weight": gaussian(seeds[11], (NK, C2), C2 ** -0.5, 1.0),
        "tensor_bias": gaussian(seeds[12], (NK,), 0.5, 3.0, (), jnp.float32),
    }


def conv_forward(inputs, kernel, stride, padding):
    return lax.conv_general_dilated(inputs, kernel, (stride, stride, stride), padding, dimension_numbers=('NCDHW', 'OIDHW', 'NCDHW'), preferred_element_type=jnp.float32)

def kernel_grad(inputs, cotangent, stride, padding):
    pad_spans = []
    for spatial in range(3):
        low_pad = padding[spatial][0]
        pad_spans.append((low_pad, 3 + stride * (cotangent.shape[2 + spatial] - 1) - inputs.shape[2 + spatial] - low_pad))
    result = lax.conv_general_dilated(inputs, cotangent, (1, 1, 1), pad_spans, rhs_dilation=(stride, stride, stride), dimension_numbers=('CNDHW', 'IODHW', 'NCDHW'), preferred_element_type=jnp.float32)
    return jnp.transpose(result, (1, 0, 2, 3, 4))

def input_grad(cotangent, kernel, stride, padding, lengths):
    pad_spans = []
    for spatial in range(3):
        low_pad = padding[spatial][0]
        pad_spans.append((2 - low_pad, lengths[spatial] - 1 - stride * (cotangent.shape[2 + spatial] - 1) + low_pad))
    flipped = kernel[:, :, ::-1, ::-1, ::-1]
    return lax.conv_general_dilated(cotangent, flipped, (1, 1, 1), pad_spans, lhs_dilation=(stride, stride, stride), dimension_numbers=('NCDHW', 'IODHW', 'NCDHW'), preferred_element_type=jnp.float32)

def record_pass(records, flux_goal, tensor_goal, mask, weights, flux_count, tensor_count):
    w_first, b_first, w_second, b_second, w_short, w_flux, b_flux, w_tensor, b_tensor = weights
    inputs = records[:, None]
    pad_first = ((1, 1), (1, 1), (1, 1))
    z_first = conv_forward(inputs, w_first, 1, pad_first) + b_first[None, :, None, None, None]
    a_first = jnp.maximum(z_first, 0.0).astype(jnp.bfloat16)
    pad_second = ((1, 0), (1, 0), (1, 0))
    even_cells = a_first[:, :, ::2, ::2, ::2]
    z_second = conv_forward(a_first, w_second, 2, pad_second) + b_second[None, :, None, None, None]
    z_second = z_second + jnp.einsum('oc,rczyx->rozyx', w_short.astype(jnp.float32), even_cells.astype(jnp.float32))
    a_second = jnp.maximum(z_second, 0.0).astype(jnp.bfloat16)
    flux_full = jnp.einsum('fo,rozyx->rfzyx', w_flux.astype(jnp.float32), a_second.astype(jnp.float32)) + b_flux[None, :, None, None, None]
    cell_count = a_second.shape[2] * a_second.shape[3] * a_second.shape[4]
    pooled = lax.optimization_barrier(jnp.sum(a_second, axis=(2, 3, 4), dtype=jnp.float32)) / cell_count
    tensor_full = jnp.dot(pooled, w_tensor.astype(jnp.float32).T, precision=lax.Precision.HIGHEST) + b_tensor[None, :]
    weight_mask = mask.astype(jnp.float32)
    flux_out = (flux_full * weight_mask[:, None, None, None, None]).astype(jnp.bfloat16)
    tensor_out = (tensor_full * weight_mask[:, None]).astype(jnp.bfloat16)
    d_flux = (2.0 / flux_count * (flux_full - flux_goal.astype(jnp.float32)) * weight_mask[:, None, None, None, None]).astype(jnp.bfloat16)
    d_tensor = 2.0 / tensor_count * (tensor_full - tensor_goal.astype(jnp.float32)) * weight_mask[:, None]
    g_flux = jnp.einsum('rfzyx,rozyx->fo', d_flux.astype(jnp.float32), a_second.astype(jnp.float32))
    g_flux_bias = lax.optimization_barrier(jnp.sum(d_flux, axis=(0, 2, 3, 4), dtype=jnp.float32))
    g_tensor = jnp.dot(d_tensor.T, pooled, precision=lax.Precision.HIGHEST)
    g_tensor_bias = lax.optimization_barrier(jnp.sum(d_tensor, axis=0))
    d_pooled = jnp.dot(d_tensor, w_tensor.astype(jnp.float32), precision=lax.Precision.HIGHEST)
    da_second = jnp.einsum('fo,rfzyx->rozyx', w_flux.astype(jnp.float32), d_flux.astype(jnp.float32)) + (d_pooled / cell_count)[:, :, None, None, None]
    dz_second = jnp.where(a_second > 0, da_second, 0.0).astype(jnp.bfloat16)
    g_second = kernel_grad(a_first, dz_second, 2, pad_second)
    g_second_bias = lax.optimization_barrier(jnp.sum(dz_second, axis=(0, 2, 3, 4), dtype=jnp.float32))
    g_short = jnp.einsum('rozyx,rczyx->oc', dz_second.astype(jnp.float32), even_cells.astype(jnp.float32))
    da_first = input_grad(dz_second, w_second, 2, pad_second, a_first.shape[2:])
    shortcut = jnp.einsum('oc,rozyx->rczyx', w_short.astype(jnp.float32), dz_second.astype(jnp.float32))
    da_first = da_first.at[:, :, ::2, ::2, ::2].add(shortcut)
    dz_first = jnp.where(a_first > 0, da_first, 0.0).astype(jnp.bfloat16)
    g_first = kernel_grad(inputs, dz_first, 1, pad_first)
    g_first_bias = lax.optimization_barrier(jnp.sum(dz_first, axis=(0, 2, 3, 4), dtype=jnp.float32))
    terms = (g_first, g_first_bias, g_second, g_second_bias, g_short, g_flux, g_flux_bias, g_tensor, g_tensor_bias)
    return ((flux_out, tensor_out), terms)

def reference(volume, flux_target, tensor_target, dest, first_weight, first_bias, second_weight, second_bias, short_weight, flux_weight, flux_bias, tensor_weight, tensor_bias):
    weights = (first_weight, first_bias, second_weight, second_bias, short_weight, flux_weight, flux_bias, tensor_weight, tensor_bias)
    live = dest >= 0
    flux_count = RECORDS * NF * ZH * YH * XH
    tensor_count = RECORDS * NK
    blocks = RECORDS // R

    def step(totals, items):
        records, flux_goal, tensor_goal, mask = items
        outputs, terms = record_pass(records, flux_goal, tensor_goal, mask, weights, flux_count, tensor_count)
        return (jax.tree.map(jnp.add, totals, terms), outputs)
    items = (volume.reshape((blocks, R) + volume.shape[1:]), flux_target.reshape((blocks, R) + flux_target.shape[1:]), tensor_target.reshape((blocks, R, NK)), live.reshape((blocks, R)))
    initial = tuple((jnp.zeros(weight.shape, jnp.float32) for weight in weights))
    totals, outputs = lax.scan(step, initial, items)
    flux_owner = outputs[0].reshape(flux_target.shape)
    tensor_owner = outputs[1].reshape(tensor_target.shape)
    target_slot = jnp.where(live, dest, RECORDS).astype(jnp.int32)
    source = jnp.zeros((RECORDS,), jnp.int32).at[target_slot].set(jnp.arange(RECORDS, dtype=jnp.int32), mode='drop')
    present = jnp.zeros((RECORDS,), jnp.bool_).at[target_slot].set(True, mode='drop')
    flux_pred = jnp.where(present[:, None, None, None, None], flux_owner[source], jnp.zeros((), flux_owner.dtype))
    tensor_pred = jnp.where(present[:, None], tensor_owner[source], jnp.zeros((), tensor_owner.dtype))
    return (flux_pred, tensor_pred, totals[0], totals[1], totals[2], totals[3], totals[4], totals[5], totals[6], totals[7], totals[8])
```

```python
import functools

import jax
import jax.numpy as jnp
from jax import lax
from jax.experimental import pallas as pl
from jax.experimental.pallas import tpu as pltpu
from jax.sharding import PartitionSpec as P

F32 = jnp.float32
BF16 = jnp.bfloat16
NN = (((1,), (0,)), ((), ()))
NT = (((1,), (1,)), ((), ()))
TN = (((0,), (0,)), ((), ()))

BLOCK = 144
CELLS = 512
TAPS = 144
CHUNK = 18
SENT = 25
ROUTED = 32


def mxu(a, b, dims=NN):
    return lax.dot_general(a, b, dims, preferred_element_type=F32)


def lanes(shape):
    return lax.broadcasted_iota(jnp.int32, shape, len(shape) - 1)


def rows(shape):
    return lax.broadcasted_iota(jnp.int32, shape, len(shape) - 2)


def pack(place_ref, vol_ref, ft_ref, out_ref):
    odd = place_ref[0] % 2 == 1
    for z in range(2):
        out_ref[:, z * 8 : z * 8 + 8, :] = vol_ref[:, z]
    goal = ft_ref[...].astype(F32)
    none = jnp.zeros_like(goal)
    low = jnp.concatenate([goal, none], axis=3)
    high = jnp.concatenate([none, goal], axis=3)
    both = jnp.where(odd, high, low)
    both = jnp.concatenate([both, jnp.zeros_like(both)], axis=2)
    out_ref[:, 16:40, :] = both.reshape(8, 24, 128).astype(BF16)


def prepare(
    w1_ref, w2_ref, ws_ref, wf_ref, wt_ref, b1_ref, b2_ref, bt_ref,
    t1_ref, w2a_ref, wb_ref, wsb_ref, fw_ref, fwt_ref, cols_ref, wtt_ref,
    base, order,
):
    base[...] = jnp.zeros_like(base)
    for kz in range(3):
        for ky in range(3):
            for kx in range(3):
                at = kz * 32 + kx * 8 + ky
                base[at : at + 1, 0:16] = w1_ref[kz, ky, kx : kx + 1, :].astype(F32)
    taps = base[0:88]
    placed = jnp.zeros((128, 128), F32)
    for px in range(2):
        for z in range(2):
            down, right = z * 32 + px * 8, px * 32 + z * 16
            parts = [pltpu.roll(taps, right, 1) if right else taps]
            if down < 40:
                parts = parts + [jnp.zeros((40 - down, 128), F32)]
            if down:
                parts = [jnp.zeros((down, 128), F32)] + parts
            placed = placed + jnp.concatenate(parts, axis=0)
    across = jnp.transpose(placed)[0:64]
    place = lanes((64, 128)) % 8
    for y in range(8):
        own = across
        if y == 0:
            own = jnp.where(place == 0, 0.0, own)
        if y == 7:
            own = jnp.where(place == 2, 0.0, own)
        if y != 1:
            own = pltpu.roll(own, (y - 1) % 128, 1)
        t1_ref[y * 64 : y * 64 + 64, :] = own.astype(BF16)
    order[...] = jnp.zeros_like(order)
    w2 = w2_ref[...].astype(F32)
    for ky in range(3):
        for s, kx in enumerate((1, 2, 0)):
            for zo, kz in enumerate((1, 2, 0)):
                to, at = ky * 144 + s * 48 + zo * 16, ((kz * 3 + ky) * 3 + kx) * 16
                order[to : to + 16, 0:32] = w2[at : at + 16]
    order[432:448, 0:32] = ws_ref[...].astype(F32)
    w2t = order[...]
    w2a_ref[...] = jnp.transpose(w2t)[0:32].astype(BF16)
    wsb_ref[...] = w2t[432:448].astype(BF16)
    own, near = ((1, 0),), ((2, 0), (0, 1))
    for sub in range(2):
        for px in range(2):
            for z in range(2):
                sides = [jnp.zeros((16, 128), F32), jnp.zeros((16, 128), F32)]
                for ky, sy in near if sub else own:
                    for kx, sx in near if px else own:
                        for kz, sz in near if z else own:
                            at = ky * 144 + (1, 2, 0).index(kx) * 48 + (1, 2, 0).index(kz) * 16
                            to = sz * 64 + sx * 32
                            part = w2t[at : at + 16]
                            sides[sy] = sides[sy] + (pltpu.roll(part, to, 1) if to else part)
                to = sub * 64 + px * 32 + z * 16
                wb_ref[to : to + 16, :] = jnp.concatenate(sides, axis=1).astype(BF16)
    base[...] = jnp.zeros_like(base)
    base[0:3, 0:32] = wf_ref[...].astype(F32)
    wide = base[0:8, :]
    wide = wide + pltpu.roll(wide, 32, 1)
    wide = wide + pltpu.roll(wide, 64, 1)
    head = jnp.concatenate(
        [jnp.broadcast_to(wide[f : f + 1], (8, 128)) for f in range(3)]
        + [jnp.zeros((104, 128), F32)],
        axis=0,
    )
    mine = (lanes((128, 128)) // 32 == rows((128, 128)) % 8) & (rows((128, 128)) < 24)
    head = jnp.where(mine, head, 0.0)
    fw_ref[...] = head[0:32].astype(BF16)
    fwt_ref[...] = jnp.transpose(head).astype(BF16)
    base[...] = jnp.zeros_like(base)
    base[0:1, 0:16] = b1_ref[...]
    base[1:2, 0:32] = b2_ref[...]
    base[8:14, 0:32] = wt_ref[...].astype(F32)
    pad = jnp.zeros((120, 128), F32)
    cols_ref[...] = jnp.transpose(jnp.concatenate([base[0:8, :], pad], axis=0))
    wtt_ref[0:32] = jnp.transpose(jnp.concatenate([base[8:16, :], pad], axis=0))[0:32]
    wtt_ref[32:40] = jnp.zeros((8, 128), F32)
    wtt_ref[32:33, 0:6] = bt_ref[...]


def step(
    flux_scale, tensor_scale, cell_count,
    place_ref, dest_ref, bf_ref, got_ref, kt_ref,
    t1_ref, w2a_ref, wb_ref, wsb_ref, fw_ref, fwt_ref, cols_ref, wtt_ref,
    out_ref,
    a_ref, a2_ref, d_ref, goal, g1, total,
):
    place = place_ref[0]
    live = jnp.where(dest_ref[place] >= 0, 1.0, 0.0)
    empty = jnp.zeros((8, 128), F32)

    def plane(z):
        if z < 0 or z > 15:
            return empty
        at = (z % 2) * 8
        return got_ref[z // 2, at : at + 8, :].astype(F32)

    low = jnp.concatenate([plane(4 * q - 1 + zi) for zi in range(4) for q in range(4)], axis=0)
    high = jnp.concatenate([plane(4 * q + 1 + zi) for zi in range(4) for q in range(4)], axis=0)
    cells = jnp.concatenate([low, high], axis=1).astype(BF16)
    r, c = rows((256, CELLS)), lanes((256, CELLS))
    x = 2 * (c % 64) - 1 + c // 128
    pick = (r % 128 == x) & (r // 128 == (c % 128) // 64)
    apart = mxu(cells, jnp.where(pick, 1.0, 0.0).astype(BF16))
    lines = []
    for zi in range(4):
        for xt in range(4):
            lines.append(
                jnp.concatenate(
                    [
                        apart[zi * 32 + q * 8 : zi * 32 + q * 8 + 8, xt * 128 : xt * 128 + 128]
                        for q in range(4)
                    ],
                    axis=1,
                )
            )
    lines.append(jnp.where(rows((16, CELLS)) == 0, 1.0, 0.0))
    xcol = jnp.concatenate(lines, axis=0).astype(BF16)
    b1 = jnp.concatenate([cols_ref[0:16, 0:1]] * 4, axis=0)
    first_z = lanes((16, CELLS)) < 64
    first_x = lanes((48, CELLS)) % 64 == 0
    a_ref[0:BLOCK] = jnp.zeros((BLOCK, CELLS), BF16)
    for y in range(8):
        z1 = mxu(t1_ref[y * 64 : y * 64 + 64], xcol[0:128]) + b1
        act = jnp.maximum(z1, 0.0).astype(BF16)
        wide = act.astype(F32)
        at = (y + 1) * BLOCK
        for px in range(2):
            moved = pltpu.roll(wide[px * 32 + 16 : px * 32 + 32], 64, 1)
            moved = jnp.where(first_z, 0.0, moved)
            a_ref[at + px * 48 : at + px * 48 + 32] = act[px * 32 : px * 32 + 32]
            a_ref[at + px * 48 + 32 : at + px * 48 + 48] = moved.astype(BF16)
        late = jnp.concatenate([wide[32:64], moved], axis=0)
        late = jnp.where(first_x, 0.0, pltpu.roll(late, 1, 1))
        a_ref[at + 96 : at + BLOCK] = late.astype(BF16)
    b2 = cols_ref[0:32, 1:2]
    pooled = jnp.zeros((32, 1), F32)
    for y in range(4):
        at = 2 * y * BLOCK
        z2 = mxu(w2a_ref[:, 0:432], a_ref[at : at + 432])
        short = mxu(w2a_ref[:, 432:448], a_ref[at + BLOCK : at + BLOCK + 16])
        z2 = (z2 + b2) + short
        act = jnp.maximum(z2, 0.0).astype(BF16)
        a2_ref[y * 32 : y * 32 + 32] = act
        pooled = pooled + jnp.sum(act.astype(F32), axis=1, keepdims=True)
    pooled = pooled / cell_count
    a2 = a2_ref[...]
    head = wtt_ref[0:32]
    tensor = jnp.sum(head * pooled, axis=0, keepdims=True) + wtt_ref[32:33]
    goal[0:8] = jnp.zeros((8, 128), F32)
    goal[0:8, 0:6] = kt_ref[...].astype(F32)
    wanted = jnp.sum(jnp.where(rows((8, 128)) == place, goal[0:8], 0.0), axis=0, keepdims=True)
    dt = tensor_scale * (tensor - wanted) * live
    spread = jnp.sum(head * dt, axis=1, keepdims=True) / cell_count
    row = rows((24, 1))
    bias = jnp.where(row < 8, bf_ref[0], jnp.where(row < 16, bf_ref[1], bf_ref[2]))
    full = mxu(fw_ref[0:24], a2) + bias
    wanted = jnp.concatenate(
        [
            got_ref[2 * q, 16:40, :].astype(F32) + got_ref[2 * q + 1, 16:40, :].astype(F32)
            for q in range(4)
        ],
        axis=1,
    )
    diff = flux_scale * (full - wanted) * live
    df = jnp.where(row % 8 < 4, diff, 0.0)
    df = jnp.concatenate([df, jnp.zeros((8, CELLS), F32)], axis=0).astype(BF16)
    member = lanes((8, CELLS)) // 64 == rows((8, CELLS))
    shares = []
    for f in range(3):
        for y in range(4):
            line = jnp.where(member, full[f * 8 + y : f * 8 + y + 1], 0.0)
            line = (line[:, 0:128] + line[:, 128:256]) + (line[:, 256:384] + line[:, 384:512])
            shares.append(line + pltpu.roll(line, 64, 1))
    left = lanes((8, 128)) < 64
    for k in range(6):
        both = jnp.where(left, shares[2 * k], shares[2 * k + 1])
        out_ref[:, CHUNK + k, :] = both.astype(BF16).astype(F32)
    tensor = tensor.astype(BF16).astype(F32)
    out_ref[:, CHUNK + 6, :] = jnp.broadcast_to(tensor, (8, 128))
    last_x = lanes((32, CELLS)) % 64 == 63
    last_z = lanes((32, CELLS)) >= 448
    bias2 = jnp.zeros((32, 1), F32)
    dz2 = []
    for y in range(4):
        da2 = mxu(fwt_ref[y * 32 : y * 32 + 32, 0:32], df) + spread
        d = jnp.where(a2_ref[y * 32 : y * 32 + 32] > 0, da2, 0.0).astype(BF16)
        wide = d.astype(F32)
        bias2 = bias2 + jnp.sum(wide, axis=1, keepdims=True)
        next_x = jnp.where(last_x, 0.0, pltpu.roll(wide, CELLS - 1, 1))
        next_z = jnp.where(last_z, 0.0, pltpu.roll(wide, CELLS - 64, 1))
        both = jnp.where(last_z, 0.0, pltpu.roll(next_x, CELLS - 64, 1))
        d_ref[y * 128 : y * 128 + 32] = d
        d_ref[y * 128 + 32 : y * 128 + 64] = next_x.astype(BF16)
        d_ref[y * 128 + 64 : y * 128 + 96] = next_z.astype(BF16)
        d_ref[y * 128 + 96 : y * 128 + 128] = both.astype(BF16)
        dz2.append(d)
    d_ref[512:640] = jnp.zeros((128, CELLS), BF16)
    none = jnp.zeros((32, CELLS), BF16)
    second = jnp.zeros((BLOCK, 128), F32)
    fold = jnp.zeros((128, 64), F32)
    tail = jnp.zeros((1, 64), F32)
    place8 = rows((128, 64)) % 8
    for y in range(4):
        at = (2 * y + 1) * BLOCK
        da1 = mxu(wb_ref[...], d_ref[y * 128 : y * 128 + 256])
        short = mxu(wsb_ref[:, 0:32], dz2[y])
        da1 = jnp.concatenate([da1[0:16] + short, da1[16:128]], axis=0)
        for sub in range(2):
            act = a_ref[at + sub * BLOCK : at + sub * BLOCK + BLOCK]
            if sub == 0:
                sides = [none, dz2[y], none, none]
            else:
                sides = [dz2[y + 1] if y < 3 else none, none, dz2[y], none]
            second = second + mxu(act, jnp.concatenate(sides, axis=0), NT)
            on = jnp.concatenate([act[0:32], act[48:80]], axis=0) > 0
            dz1 = jnp.where(on, da1[sub * 64 : sub * 64 + 64], 0.0).astype(BF16)
            part = mxu(xcol, dz1, NT)
            tail = tail + part[128:129]
            part = part[0:128]
            shift = 2 * y + sub - 1
            if shift == -1:
                part = jnp.where(place8 == 7, 0.0, part)
            if shift == 6:
                part = jnp.where(place8 == 0, 0.0, part)
            if shift:
                part = pltpu.roll(part, (-shift) % 128, 0)
            fold = fold + part
    g1[...] = jnp.zeros_like(g1)
    g1[0:128, 0:64] = fold
    g1[128:129, 0:64] = tail
    first = jnp.zeros((88, 128), F32)
    first_bias = jnp.zeros((1, 128), F32)
    for px in range(2):
        for z in range(2):
            down, right = z * 32 + px * 8, px * 32 + z * 16
            to = (96 - right) % 128
            first = first + pltpu.roll(g1[down : down + 88, :], to, 1)
            first_bias = first_bias + pltpu.roll(g1[128:129, :], to, 1)
    cross = mxu(df, a2, NT)
    same = lanes((32, 128)) // 32 == rows((32, 128)) % 8
    cross = jnp.where(same, cross, 0.0)
    cross = cross + pltpu.roll(cross, 64, 1)
    cross = cross + pltpu.roll(cross, 32, 1)
    flux_sum = jnp.sum(df.astype(F32), axis=1, keepdims=True)
    lane = lanes((1, 128))
    total[...] = second
    total[0:88] = second[0:88] + jnp.where((lane >= 96) & (lane < 112), first, 0.0)
    total[96:128] = second[96:128] + jnp.where(lane >= 96, pltpu.roll(pooled * dt, 96, 1), 0.0)
    kept = lane >= 96
    bias_row = jnp.zeros((1, 128), F32)
    for f in range(3):
        line = jnp.sum(cross[f * 8 : f * 8 + 8], axis=0, keepdims=True)
        total[128 + f : 129 + f] = second[128 + f : 129 + f] + jnp.where(kept, line, 0.0)
        sums = jnp.sum(flux_sum[f * 8 : f * 8 + 8], axis=0, keepdims=True)
        bias_row = jnp.where(lane == 96 + f, sums, bias_row)
    total[131:132] = second[131:132] + bias_row
    total[132:133] = second[132:133] + jnp.where(kept, pltpu.roll(dt, 96, 1), 0.0)
    total[133:134] = second[133:134] + jnp.where(kept & (lane < 112), first_bias, 0.0)
    column = jnp.concatenate([jnp.zeros((96, 1), F32), bias2], axis=0)
    column = jnp.transpose(jnp.broadcast_to(column, (128, 128)))[0:1]
    total[134:135] = second[134:135] + column
    for p in range(8):
        out_ref[p, 0:CHUNK] = total[p * CHUNK : p * CHUNK + CHUNK]


def route(dest_ref, got_ref, out_ref):
    chunk = got_ref[0, 0:CHUNK]
    for s in range(1, 8):
        chunk = chunk + got_ref[s, 0:CHUNK]
    groups = out_ref.shape[0]
    out_ref[:, 0:CHUNK, :] = jnp.broadcast_to(chunk[None], (groups, CHUNK, 128))
    lane = lanes((7, 128))
    marked = (lane == 127) & (rows((7, 128)) == 6)
    blank = jnp.where(marked, -1.0, 0.0)
    for w in range(2):
        at = CHUNK + 7 * w
        out_ref[:, at : at + 7, :] = jnp.broadcast_to(blank[None], (groups, 7, 128))
    for r in range(8):
        dest = dest_ref[r]
        group = dest // 8
        earlier = jnp.int32(0)
        for e in range(r):
            twin = (dest_ref[e] >= 0) & (dest_ref[e] // 8 == group)
            earlier = earlier + jnp.where(twin, 1, 0)
        slot = (dest % 8).astype(F32)
        piece = jnp.where(marked, slot, got_ref[r, CHUNK : CHUNK + 7])

        @pl.when((dest >= 0) & (earlier == 0))
        def _():
            out_ref[group, CHUNK : CHUNK + 7, :] = piece

        @pl.when((dest >= 0) & (earlier > 0))
        def _():
            out_ref[group, CHUNK + 7 : CHUNK + 14, :] = piece


def spread(got_ref, out_ref):
    chunk = jnp.sum(got_ref[:, 0:CHUNK, :], axis=0)
    out_ref[...] = jnp.broadcast_to(chunk[None], out_ref.shape)


def place_records(got_ref, fp_ref, tp_ref):
    count = got_ref.shape[0]

    def candidates(k):
        return jnp.concatenate(
            [got_ref[:, CHUNK + k, :], got_ref[:, CHUNK + 7 + k, :]], axis=0
        )

    last = candidates(6)
    lane = lanes((2 * count, 128))
    slot = jnp.sum(jnp.where(lane == 127, last, 0.0), axis=1, keepdims=True)
    hit = jnp.where((slot == lane.astype(F32)) & (lane < 8), 1.0, 0.0)
    hit = jnp.concatenate([hit, jnp.zeros((128 - 2 * count, 128), F32)], axis=0)
    choose = jnp.transpose(hit)[0:8, 0 : 2 * count].astype(BF16)
    for k in range(6):
        got = mxu(choose, candidates(k).astype(BF16)).astype(BF16)
        f, y = (2 * k) // 4, (2 * k) % 4
        fp_ref[:, f, y, :] = got[:, 0:64]
        fp_ref[:, f, y + 1, :] = got[:, 64:128]
    tp_ref[...] = mxu(choose, last.astype(BF16))[:, 0:6].astype(BF16)


def finish(
    got_ref,
    g1_ref, b1_ref, g2_ref, b2_ref, gs_ref, gf_ref, bf_ref, gt_ref, bt_ref,
    total,
):
    for p in range(8):
        total[p * CHUNK : p * CHUNK + CHUNK] = got_ref[p]
    for kz in range(3):
        for ky in range(3):
            for kx in range(3):
                at = kz * 32 + kx * 8 + ky
                g1_ref[(kz * 3 + ky) * 3 + kx] = total[at : at + 1, 96:112]
    for ky in range(3):
        block = total[0:144, ky * 32 : ky * 32 + 32]
        for s, kx in enumerate((1, 2, 0)):
            for zo, kz in enumerate((1, 2, 0)):
                to = ((kz * 3 + ky) * 3 + kx) * 16
                part = block[s * 48 + zo * 16 : s * 48 + zo * 16 + 16]
                g2_ref[to : to + 16] = part
                if ky == 1 and kx == 1 and kz == 1:
                    gs_ref[...] = part
    heads = jnp.concatenate([total[96:128, :], jnp.zeros((96, 128), F32)], axis=0)
    gt_ref[...] = jnp.transpose(heads)[96:102, 0:32]
    gf_ref[...] = total[128:131, 96:128]
    bf_ref[...] = total[131:132, 96:99]
    bt_ref[...] = total[132:133, 96:102]
    b1_ref[...] = total[133:134, 96:112]
    b2_ref[...] = total[134:135, 96:128]


SMEM = pl.BlockSpec(memory_space=pltpu.SMEM)
VMEM = pl.BlockSpec(memory_space=pltpu.VMEM)
LIMIT = 48 * 1024 * 1024


def run(kernel, name, scalars, arrays, outs, scratch=()):
    return pl.pallas_call(
        kernel,
        out_shape=tuple(jax.ShapeDtypeStruct(s, t) for s, t in outs),
        in_specs=[SMEM] * len(scalars) + [VMEM] * len(arrays),
        out_specs=(VMEM,) * len(outs),
        scratch_shapes=[pltpu.VMEM(s, t) for s, t in scratch],
        compiler_params=pltpu.CompilerParams(vmem_limit_bytes=LIMIT),
        name=name,
    )(*scalars, *arrays)


def exchange(block, axis):
    return lax.all_to_all(block, axis, 0, 0, tiled=True)


def on_device(
    volume, flux_target, tensor_target, dest,
    first_weight, first_bias, second_weight, second_bias, short_weight,
    flux_weight, flux_bias, tensor_weight, tensor_bias,
):
    groups, slabs = lax.axis_size("dp"), lax.axis_size("slab")
    records = 8 * groups
    flux_count = records * 3 * slabs * 4 * 64
    tensor_count = records * 6
    cell_count = slabs * 4 * 64
    place = lax.axis_index("slab").astype(jnp.int32).reshape(1)
    (mine,) = run(
        pack, "pack", [place], [volume, flux_target[:, :, 0]], [((8, 40, 128), BF16)]
    )
    record = exchange(mine, "slab")
    weights = run(
        prepare, "prepare", [],
        [
            jnp.transpose(first_weight[:, 0], (1, 2, 3, 0)),
            jnp.transpose(second_weight, (2, 3, 4, 1, 0)).reshape(432, 32),
            jnp.transpose(short_weight),
            flux_weight, tensor_weight,
            first_bias.reshape(1, 16), second_bias.reshape(1, 32), tensor_bias.reshape(1, 6),
        ],
        [
            ((512, 128), BF16), ((32, 512), BF16), ((128, 256), BF16), ((16, 128), BF16),
            ((32, 128), BF16), ((128, 128), BF16), ((128, 128), F32), ((40, 128), F32),
        ],
        [((96, 128), F32), ((512, 128), F32)],
    )
    (terms,) = run(
        functools.partial(step, 2.0 / flux_count, 2.0 / tensor_count, float(cell_count)),
        "step", [place, dest, flux_bias], [record, tensor_target, *weights],
        [((8, SENT, 128), F32)],
        [
            ((9 * BLOCK, CELLS), BF16), ((128, CELLS), BF16), ((640, CELLS), BF16),
            ((8, 128), F32), ((136, 128), F32), ((BLOCK, 128), F32),
        ],
    )
    terms = exchange(terms, "slab")
    (routed,) = run(route, "route", [dest], [terms], [((groups, ROUTED, 128), F32)])
    routed = exchange(routed, "dp")
    (chunk,) = run(spread, "spread", [], [routed], [((slabs, CHUNK, 128), F32)])
    total = exchange(chunk, "slab")
    fp, tp = run(
        place_records, "place", [], [routed], [((8, 3, 4, 64), BF16), ((8, 6), BF16)]
    )
    g1, b1, g2, b2, gs, gf, bf, gt, bt = run(
        finish, "finish", [], [total],
        [
            ((27, 1, 16), F32), ((1, 16), F32), ((432, 32), F32), ((1, 32), F32),
            ((16, 32), F32), ((3, 32), F32), ((1, 3), F32), ((6, 32), F32), ((1, 6), F32),
        ],
        [((BLOCK, 128), F32)],
    )
    return (
        fp[:, :, None],
        tp,
        jnp.transpose(g1.reshape(3, 3, 3, 1, 16), (4, 3, 0, 1, 2)),
        b1.reshape(16),
        jnp.transpose(g2.reshape(3, 3, 3, 16, 32), (4, 3, 0, 1, 2)),
        b2.reshape(32),
        jnp.transpose(gs),
        gf,
        bf.reshape(3),
        gt,
        bt.reshape(6),
    )


def solution(mesh):
    cells = P("dp", "slab", None, None)
    fields = P("dp", None, "slab", None, None)
    return jax.shard_map(
        on_device,
        mesh=mesh,
        in_specs=(cells, fields, P("dp", None), P("dp")) + (P(),) * 9,
        out_specs=(fields, P("dp", None)) + (P(),) * 9,
        check_vma=False,
    )
```

```python
import functools

import jax
import jax.numpy as jnp
from jax import lax
from jax.experimental import pallas as pl
from jax.experimental.pallas import tpu as pltpu
from jax.sharding import PartitionSpec as P

F32 = jnp.float32
BF16 = jnp.bfloat16
NN = (((1,), (0,)), ((), ()))
NT = (((1,), (1,)), ((), ()))
TN = (((0,), (0,)), ((), ()))

BLOCK = 144
CELLS = 512
TAPS = 144
ROWS = 128
LAYERS = 64


def mxu(a, b, dims=NN):
    return lax.dot_general(a, b, dims, preferred_element_type=F32)


def lanes(shape):
    return lax.broadcasted_iota(jnp.int32, shape, len(shape) - 1)


def rows(shape):
    return lax.broadcasted_iota(jnp.int32, shape, len(shape) - 2)


def pack(place_ref, vol_hbm, ft_hbm, out_ref, vol_ref, ft_ref, done):
    copies = [
        pltpu.make_async_copy(vol_hbm, vol_ref, done.at[0]),
        pltpu.make_async_copy(ft_hbm, ft_ref, done.at[1]),
    ]
    for copy in copies:
        copy.start()
    odd = place_ref[0] % 2 == 1
    copies[0].wait()
    for z in range(2):
        out_ref[:, z * 8 : z * 8 + 8, :] = vol_ref[:, z]
    copies[1].wait()
    goal = ft_ref[...].astype(F32)
    none = jnp.zeros_like(goal)
    low = jnp.concatenate([goal, none], axis=3)
    high = jnp.concatenate([none, goal], axis=3)
    both = jnp.where(odd, high, low)
    both = jnp.concatenate([both, jnp.zeros_like(both)], axis=2)
    out_ref[:, 16:40, :] = both.reshape(8, 24, 128).astype(BF16)


def prepare(
    place_ref, dest_ref, bf_ref,
    w1_ref, w2_ref, ws_ref, wf_ref, wt_ref, b1_ref, b2_ref, bt_ref, kt_ref,
    t1_ref, w2a_ref, wb_ref, wsb_ref, fw_ref, fwt_ref, cols_ref, wtt_ref, pick_ref,
    base, order,
    *, breadth,
):
    r, c = rows((256, CELLS)), lanes((256, CELLS))
    x = 2 * (c % 64) - 1 + c // 128
    pick = (r % 128 == x) & (r // 128 == (c % 128) // 64)
    pick_ref[...] = jnp.where(pick, 1.0, 0.0).astype(BF16)
    base[...] = jnp.zeros_like(base)
    for kz in range(3):
        for ky in range(3):
            for kx in range(3):
                at = kz * 32 + kx * 8 + ky
                base[at : at + 1, 0:16] = w1_ref[kz, ky, kx : kx + 1, :].astype(F32)
    taps = base[0:88]
    placed = jnp.zeros((128, 128), F32)
    for px in range(2):
        for z in range(2):
            down, right = z * 32 + px * 8, px * 32 + z * 16
            parts = [pltpu.roll(taps, right, 1) if right else taps]
            if down < 40:
                parts = parts + [jnp.zeros((40 - down, 128), F32)]
            if down:
                parts = [jnp.zeros((down, 128), F32)] + parts
            placed = placed + jnp.concatenate(parts, axis=0)
    across = jnp.transpose(placed)[0:64]
    place = lanes((64, 128)) % 8
    for y in range(8):
        own = across
        if y == 0:
            own = jnp.where(place == 0, 0.0, own)
        if y == 7:
            own = jnp.where(place == 2, 0.0, own)
        if y != 1:
            own = pltpu.roll(own, (y - 1) % 128, 1)
        t1_ref[y * 64 : y * 64 + 64, :] = own.astype(BF16)
    order[...] = jnp.zeros_like(order)
    w2 = w2_ref[...].astype(F32)
    for ky in range(3):
        for s, kx in enumerate((1, 2, 0)):
            for zo, kz in enumerate((1, 2, 0)):
                to, at = ky * 144 + s * 48 + zo * 16, ((kz * 3 + ky) * 3 + kx) * 16
                order[to : to + 16, 0:32] = w2[at : at + 16]
    order[432:448, 0:32] = ws_ref[...].astype(F32)
    w2t = order[...]
    w2a_ref[...] = jnp.transpose(w2t)[0:32].astype(BF16)
    wsb_ref[...] = w2t[432:448].astype(BF16)
    own, near = ((1, 0),), ((2, 0), (0, 1))
    for sub in range(2):
        for px in range(2):
            for z in range(2):
                sides = [jnp.zeros((16, 128), F32), jnp.zeros((16, 128), F32)]
                for ky, sy in near if sub else own:
                    for kx, sx in near if px else own:
                        for kz, sz in near if z else own:
                            at = ky * 144 + (1, 2, 0).index(kx) * 48 + (1, 2, 0).index(kz) * 16
                            to = sz * 64 + sx * 32
                            part = w2t[at : at + 16]
                            sides[sy] = sides[sy] + (pltpu.roll(part, to, 1) if to else part)
                to = sub * 64 + px * 32 + z * 16
                wb_ref[to : to + 16, :] = jnp.concatenate(sides, axis=1).astype(BF16)
    base[...] = jnp.zeros_like(base)
    base[0:3, 0:32] = wf_ref[...].astype(F32)
    wide = base[0:8, :]
    wide = wide + pltpu.roll(wide, 32, 1)
    wide = wide + pltpu.roll(wide, 64, 1)
    head = jnp.concatenate(
        [jnp.broadcast_to(wide[f : f + 1], (8, 128)) for f in range(3)]
        + [jnp.zeros((104, 128), F32)],
        axis=0,
    )
    mine = (lanes((128, 128)) // 32 == rows((128, 128)) % 8) & (rows((128, 128)) < 24)
    head = jnp.where(mine, head, 0.0)
    fw_ref[...] = head[0:32].astype(BF16)
    fwt_ref[...] = jnp.transpose(head).astype(BF16)
    base[...] = jnp.zeros_like(base)
    base[0:1, 0:16] = b1_ref[...]
    base[1:2, 0:32] = b2_ref[...]
    base[8:14, 0:32] = wt_ref[...].astype(F32)
    pad = jnp.zeros((120, 128), F32)
    cols_ref[...] = jnp.transpose(jnp.concatenate([base[0:8, :], pad], axis=0))
    wtt_ref[0:32] = jnp.transpose(jnp.concatenate([base[8:16, :], pad], axis=0))[0:32]
    base[16:24, 0:6] = kt_ref[...].astype(F32)
    wtt_ref[32:40] = jnp.zeros((8, 128), F32)
    wtt_ref[32:33, 0:6] = bt_ref[...]
    mine = rows((8, 128)) == place_ref[0]
    wtt_ref[33:34] = jnp.sum(jnp.where(mine, base[16:24], 0.0), axis=0, keepdims=True)
    dest = dest_ref[place_ref[0]]
    live = jnp.where(dest >= 0, 1.0, 0.0)
    wtt_ref[34:35] = jnp.broadcast_to(live, (1, 128))
    wtt_ref[35:36] = jnp.broadcast_to(dest.astype(F32), (1, 128))
    across = (jnp.maximum(dest, 0) // 8) % breadth
    for y in range(breadth):
        here = jnp.where((dest >= 0) & (across == y), 1.0, 0.0)
        wtt_ref[36 + y : 37 + y] = jnp.broadcast_to(here, (1, 128))
    row = rows((128, 1))
    bias = jnp.where(row < 8, bf_ref[0], jnp.where(row < 16, bf_ref[1], bf_ref[2]))
    cols_ref[:, 2:3] = bias


def step(
    flux_scale, tensor_scale, cell_count,
    got_ref,
    t1_ref, w2a_ref, wb_ref, wsb_ref, fw_ref, fwt_ref, cols_ref, wtt_ref, pick_ref,
    out_ref,
    a_ref, a2_ref, d_ref, dz1_ref, total, sent,
    *, breadth,
):
    live = wtt_ref[34:35, 0:1]
    empty = jnp.zeros((8, 128), F32)

    def plane(z):
        if z < 0 or z > 15:
            return empty
        at = (z % 2) * 8
        return got_ref[z // 2, at : at + 8, :].astype(F32)

    low = jnp.concatenate([plane(4 * q - 1 + zi) for zi in range(4) for q in range(4)], axis=0)
    high = jnp.concatenate([plane(4 * q + 1 + zi) for zi in range(4) for q in range(4)], axis=0)
    cells = jnp.concatenate([low, high], axis=1).astype(BF16)
    apart = mxu(cells, pick_ref[...])
    lines = []
    for zi in range(4):
        for xt in range(4):
            lines.append(
                jnp.concatenate(
                    [
                        apart[zi * 32 + q * 8 : zi * 32 + q * 8 + 8, xt * 128 : xt * 128 + 128]
                        for q in range(4)
                    ],
                    axis=1,
                )
            )
    lines.append(jnp.where(rows((16, CELLS)) == 0, 1.0, 0.0))
    xcol = jnp.concatenate(lines, axis=0).astype(BF16)
    b1 = jnp.concatenate([cols_ref[0:16, 0:1]] * 4, axis=0)
    first_z = lanes((16, CELLS)) < 64
    first_x = lanes((48, CELLS)) % 64 == 0
    a_ref[0:BLOCK] = jnp.zeros((BLOCK, CELLS), BF16)
    for y in range(8):
        z1 = mxu(t1_ref[y * 64 : y * 64 + 64], xcol[0:128]) + b1
        act = jnp.maximum(z1, 0.0).astype(BF16)
        wide = act.astype(F32)
        at = (y + 1) * BLOCK
        for px in range(2):
            moved = pltpu.roll(wide[px * 32 + 16 : px * 32 + 32], 64, 1)
            moved = jnp.where(first_z, 0.0, moved)
            a_ref[at + px * 48 : at + px * 48 + 32] = act[px * 32 : px * 32 + 32]
            a_ref[at + px * 48 + 32 : at + px * 48 + 48] = moved.astype(BF16)
        late = jnp.concatenate([wide[32:64], moved], axis=0)
        late = jnp.where(first_x, 0.0, pltpu.roll(late, 1, 1))
        a_ref[at + 96 : at + BLOCK] = late.astype(BF16)
    b2 = cols_ref[0:32, 1:2]
    pooled = jnp.zeros((32, 1), F32)
    for y in range(4):
        at = 2 * y * BLOCK
        z2 = mxu(w2a_ref[:, 0:432], a_ref[at : at + 432])
        short = mxu(w2a_ref[:, 432:448], a_ref[at + BLOCK : at + BLOCK + 16])
        z2 = (z2 + b2) + short
        act = jnp.maximum(z2, 0.0).astype(BF16)
        a2_ref[y * 32 : y * 32 + 32] = act
        pooled = pooled + jnp.sum(act.astype(F32), axis=1, keepdims=True)
    pooled = pooled / cell_count
    a2 = a2_ref[...]
    head = wtt_ref[0:32]
    tensor = jnp.sum(head * pooled, axis=0, keepdims=True) + wtt_ref[32:33]
    dt = tensor_scale * (tensor - wtt_ref[33:34]) * live
    spread = jnp.sum(head * dt, axis=1, keepdims=True) / cell_count
    row = rows((24, 1))
    full = mxu(fw_ref[0:24], a2) + cols_ref[0:24, 2:3]
    wanted = jnp.concatenate(
        [
            got_ref[2 * q, 16:40, :].astype(F32) + got_ref[2 * q + 1, 16:40, :].astype(F32)
            for q in range(4)
        ],
        axis=1,
    )
    diff = flux_scale * (full - wanted) * live
    df = jnp.where(row % 8 < 4, diff, 0.0)
    df = jnp.concatenate([df, jnp.zeros((8, CELLS), F32)], axis=0).astype(BF16)
    member = lanes((8, CELLS)) // 64 == rows((8, CELLS))
    shares = []
    for f in range(3):
        for y in range(4):
            line = jnp.where(member, full[f * 8 + y : f * 8 + y + 1], 0.0)
            line = (line[:, 0:128] + line[:, 128:256]) + (line[:, 256:384] + line[:, 384:512])
            shares.append(line + pltpu.roll(line, 64, 1))
    left = lanes((8, 128)) < 64
    marked = lanes((8, 128)) == 6
    for y in range(breadth):
        here = wtt_ref[36 + y : 37 + y] > 0
        for k in range(6):
            both = jnp.where(left, shares[2 * k], shares[2 * k + 1])
            sent[y * 8 : y * 8 + 8, 8 + k, :] = jnp.where(here, both, 0.0)
        last = jnp.where(marked, wtt_ref[35:36], jnp.broadcast_to(tensor, (8, 128)))
        none = jnp.where(marked, -1.0, 0.0)
        sent[y * 8 : y * 8 + 8, 14, :] = jnp.where(here, last, none)
        sent[y * 8 : y * 8 + 8, 15, :] = jnp.zeros((8, 128), F32)
    last_x = lanes((32, CELLS)) % 64 == 63
    last_z = lanes((32, CELLS)) >= 448
    bias2 = jnp.zeros((32, 1), F32)
    dz2 = []
    for y in range(4):
        da2 = mxu(fwt_ref[y * 32 : y * 32 + 32, 0:32], df) + spread
        d = jnp.where(a2_ref[y * 32 : y * 32 + 32] > 0, da2, 0.0).astype(BF16)
        wide = d.astype(F32)
        bias2 = bias2 + jnp.sum(wide, axis=1, keepdims=True)
        next_x = jnp.where(last_x, 0.0, pltpu.roll(wide, CELLS - 1, 1))
        next_z = jnp.where(last_z, 0.0, pltpu.roll(wide, CELLS - 64, 1))
        both = jnp.where(last_z, 0.0, pltpu.roll(next_x, CELLS - 64, 1))
        d_ref[y * 128 : y * 128 + 32] = d
        d_ref[y * 128 + 32 : y * 128 + 64] = next_x.astype(BF16)
        d_ref[y * 128 + 64 : y * 128 + 96] = next_z.astype(BF16)
        d_ref[y * 128 + 96 : y * 128 + 128] = both.astype(BF16)
        dz2.append(d)
    d_ref[512:640] = jnp.zeros((128, CELLS), BF16)
    none = jnp.zeros((32, CELLS), BF16)
    second = jnp.zeros((BLOCK, 128), F32)
    for y in range(4):
        at = (2 * y + 1) * BLOCK
        da1 = mxu(wb_ref[...], d_ref[y * 128 : y * 128 + 256])
        short = mxu(wsb_ref[:, 0:32], dz2[y])
        da1 = jnp.concatenate([da1[0:16] + short, da1[16:128]], axis=0)
        for sub in range(2):
            act = a_ref[at + sub * BLOCK : at + sub * BLOCK + BLOCK]
            if sub == 0:
                sides = [none, dz2[y], none, none]
            else:
                sides = [dz2[y + 1] if y < 3 else none, none, dz2[y], none]
            second = second + mxu(act, jnp.concatenate(sides, axis=0), NT)
            on = jnp.concatenate([act[0:32], act[48:80]], axis=0) > 0
            dz1 = jnp.where(on, da1[sub * 64 : sub * 64 + 64], 0.0).astype(BF16)
            dz1_ref[(2 * y + sub) * 64 : (2 * y + sub) * 64 + 64] = dz1
    parts = mxu(dz1_ref[...], xcol, NT)
    place8 = lanes((64, 128)) % 8
    fold = jnp.zeros((64, 128), F32)
    tail = jnp.zeros((64, 1), F32)
    for y in range(8):
        part = parts[y * 64 : y * 64 + 64, 0:128]
        tail = tail + parts[y * 64 : y * 64 + 64, 128:129]
        if y == 0:
            part = jnp.where(place8 == 7, 0.0, part)
        if y == 7:
            part = jnp.where(place8 == 0, 0.0, part)
        if y != 1:
            part = pltpu.roll(part, (1 - y) % 128, 1)
        fold = fold + part
    first = jnp.zeros((16, 128), F32)
    first_bias = jnp.zeros((16, 1), F32)
    for px in range(2):
        for z in range(2):
            at, left = px * 32 + z * 16, z * 32 + px * 8
            part = fold[at : at + 16]
            first = first + (pltpu.roll(part, 128 - left, 1) if left else part)
            first_bias = first_bias + tail[at : at + 16]
    lane = lanes((1, 128))
    bias2 = jnp.where(lanes((32, 128)) == 0, bias2, pooled * pltpu.roll(dt, 1, 1))
    upright = jnp.concatenate(
        [
            jnp.where(lanes((16, 128)) == 127, first_bias, first),
            jnp.zeros((16, 128), F32),
            bias2,
            jnp.zeros((64, 128), F32),
        ],
        axis=0,
    )
    upright = jnp.transpose(upright)
    cross = mxu(df, a2, NT)
    same = lanes((32, 128)) // 32 == rows((32, 128)) % 8
    cross = jnp.where(same, cross, 0.0)
    cross = cross + pltpu.roll(cross, 64, 1)
    cross = cross + pltpu.roll(cross, 32, 1)
    flux_sum = jnp.sum(df.astype(F32), axis=1, keepdims=True)
    total[0:108] = second[0:108]
    for ky in range(3):
        total[ky * 36 : ky * 36 + 36, 96:128] = second[108:144, ky * 32 : ky * 32 + 32]
    low = lanes((8, 128)) < 16
    small = jnp.zeros((8, 128), F32)
    for g in range(8):
        at = (g // 3) * 32 + (g % 3) * 8
        part = jnp.where(low, upright[at : at + 8], 0.0)
        small = small + (pltpu.roll(part, 16 * g, 1) if g else part)
    total[108:111] = small[0:3]
    lines = jnp.concatenate(
        [
            jnp.sum(cross[f * 8 : f * 8 + 8], axis=0, keepdims=True) for f in range(3)
        ]
        + [jnp.zeros((5, 128), F32)],
        axis=0,
    )
    lane8, row8 = lanes((8, 128)), rows((8, 128))
    last = jnp.where(low, upright[80:88], 0.0)
    last = jnp.where((lane8 >= 32) & (lane8 < 64), lines, last)
    first_bias = pltpu.roll(jnp.where(lane < 16, upright[127:128], 0.0), 64, 1)
    second_bias = pltpu.roll(jnp.where((lane >= 32) & (lane < 64), upright[0:1], 0.0), 32, 1)
    bias_row = jnp.zeros((1, 128), F32)
    for f in range(3):
        sums = jnp.sum(flux_sum[f * 8 : f * 8 + 8], axis=0, keepdims=True)
        bias_row = jnp.where(lane == 96 + f, sums, bias_row)
    tensor_bias = pltpu.roll(jnp.where(lane < 32, dt, 0.0), 64, 1)
    last = last + jnp.where(row8 == 0, second_bias + bias_row, 0.0)
    last = last + jnp.where(row8 == 1, first_bias, 0.0)
    last = last + jnp.where(row8 == 2, tensor_bias, 0.0)
    total[111:114] = last[0:3]
    total[114:120] = upright[1:7]
    total[120:128] = jnp.zeros((8, 128), F32)
    upper = rows((8, 128)) < 4
    for t in range(0, ROWS, 8):
        block = total[t : t + 8]
        high = block.astype(BF16).astype(F32)
        low = block - high
        sent[t // 4, 0:8, :] = jnp.where(upper, high, pltpu.roll(low, 4, 0))
        sent[t // 4 + 1, 0:8, :] = jnp.where(upper, pltpu.roll(high, 4, 0), low)
    out_ref[...] = sent[...].astype(BF16)


def route(got_ref, out_ref, recs, *, breadth):
    recs[...] = got_ref[...].astype(F32)
    count = got_ref.shape[0]
    depth = out_ref.shape[0]
    parts = recs[0, 0:8, :]
    for p in range(1, count):
        parts = parts + recs[p, 0:8, :]
    upper = rows((8, 128)) < 4
    full = parts + pltpu.roll(parts, 4, 0)
    high = full.astype(BF16).astype(F32)
    share = jnp.where(upper, high, full - high)
    lane = lanes((count, 128))
    last = recs[:, 14, :]
    dest = jnp.sum(jnp.where(lane == 6, last, 0.0), axis=1, keepdims=True)
    mine = lax.axis_index("y")
    slot = (lane // 8 * breadth + mine) * 8 + lane % 8
    hit = jnp.where((dest == slot.astype(F32)) & (lane < 8 * depth), 1.0, 0.0)
    if count < 128:
        hit = jnp.concatenate([hit, jnp.zeros((128 - count, 128), F32)], axis=0)
    choose = jnp.transpose(hit)[0 : 8 * depth, 0:count].astype(BF16)
    layers = [mxu(choose, recs[:, 8 + k, :].astype(BF16)) for k in range(7)]
    for z in range(depth):
        tall = [share] + [layer[z * 8 : z * 8 + 8] for layer in layers]
        out_ref[z] = jnp.concatenate(tall, axis=0).astype(BF16)


def spread(got_ref, out_ref):
    parts = jnp.sum(got_ref[...].astype(F32)[:, 0:8, :], axis=0)
    share = parts[0:4] + parts[4:8]
    out_ref[...] = jnp.broadcast_to(share[None], out_ref.shape)


def place_records(got_ref, fp_ref, tp_ref):
    layers = got_ref[0].astype(F32)
    for z in range(1, got_ref.shape[0]):
        layers = layers + got_ref[z].astype(F32)
    for k in range(6):
        got = layers[8 + 8 * k : 16 + 8 * k].astype(BF16)
        f, y = (2 * k) // 4, (2 * k) % 4
        fp_ref[:, f, y, :] = got[:, 0:64]
        fp_ref[:, f, y + 1, :] = got[:, 64:128]
    tp_ref[...] = layers[56:64, 0:6].astype(BF16)


def finish(
    got_ref,
    g1_ref, b1_ref, g2_ref, b2_ref, gs_ref, gf_ref, bf_ref, gt_ref, bt_ref,
    total, second,
):
    for p in range(got_ref.shape[0]):
        total[p * 4 : p * 4 + 4] = got_ref[p]
    for kz in range(3):
        for ky in range(3):
            for kx in range(3):
                g = kz * 3 + kx
                at, to = (108 + ky, 16 * g) if g < 8 else (111 + ky, 0)
                g1_ref[(kz * 3 + ky) * 3 + kx] = total[at : at + 1, to : to + 16]
    for ky in range(3):
        second[0:108] = total[0:108, ky * 32 : ky * 32 + 32]
        second[108:144] = total[ky * 36 : ky * 36 + 36, 96:128]
        for s, kx in enumerate((1, 2, 0)):
            for zo, kz in enumerate((1, 2, 0)):
                to = ((kz * 3 + ky) * 3 + kx) * 16
                part = second[s * 48 + zo * 16 : s * 48 + zo * 16 + 16]
                g2_ref[to : to + 16] = part
                if ky == 1 and kx == 1 and kz == 1:
                    gs_ref[...] = part
    gf_ref[...] = total[111:114, 32:64]
    b2_ref[...] = total[111:112, 64:96]
    bf_ref[...] = total[111:112, 96:99]
    b1_ref[...] = total[112:113, 64:80]
    bt_ref[...] = total[113:114, 64:70]
    gt_ref[...] = total[114:120, 32:64]


SMEM = pl.BlockSpec(memory_space=pltpu.SMEM)
VMEM = pl.BlockSpec(memory_space=pltpu.VMEM)
MIB = 1024 * 1024


def run(kernel, name, scalars, arrays, outs, scratch=(), held=None, limit=16):
    return pl.pallas_call(
        kernel,
        out_shape=tuple(jax.ShapeDtypeStruct(*o[0:2]) for o in outs),
        in_specs=[SMEM] * len(scalars) + [held or VMEM] * len(arrays),
        out_specs=tuple(o[2] if len(o) > 2 else VMEM for o in outs),
        scratch_shapes=[pltpu.VMEM(*s) if isinstance(s, tuple) else s for s in scratch],
        compiler_params=pltpu.CompilerParams(vmem_limit_bytes=limit * MIB),
        name=name,
    )(*scalars, *arrays)


def exchange(block, axis):
    return lax.all_to_all(block, axis, 0, 0, tiled=True)


def on_device(
    volume, flux_target, tensor_target, dest,
    first_weight, first_bias, second_weight, second_bias, short_weight,
    flux_weight, flux_bias, tensor_weight, tensor_bias,
):
    depth, breadth, slabs = (lax.axis_size(a) for a in ("z", "y", "slab"))
    count = breadth * slabs
    records = 8 * depth * breadth
    flux_count = records * 3 * slabs * 4 * 64
    tensor_count = records * 6
    cell_count = slabs * 4 * 64
    place = lax.axis_index("slab").astype(jnp.int32).reshape(1)
    (mine,) = run(
        pack, "pack", [place], [volume, flux_target[:, :, 0]], [((8, 40, 128), BF16)],
        [((8, 2, 8, 128), BF16), ((8, 3, 4, 64), BF16), pltpu.SemaphoreType.DMA((2,))],
        pl.BlockSpec(memory_space=pl.ANY), 60,
    )
    record = exchange(mine, "slab")
    weights = run(
        functools.partial(prepare, breadth=breadth), "prepare", [place, dest, flux_bias],
        [
            jnp.transpose(first_weight[:, 0], (1, 2, 3, 0)),
            jnp.transpose(second_weight, (2, 3, 4, 1, 0)).reshape(432, 32),
            jnp.transpose(short_weight),
            flux_weight, tensor_weight,
            first_bias.reshape(1, 16), second_bias.reshape(1, 32), tensor_bias.reshape(1, 6),
            tensor_target,
        ],
        [
            ((512, 128), BF16), ((32, 512), BF16), ((128, 256), BF16), ((16, 128), BF16),
            ((32, 128), BF16), ((128, 128), BF16), ((128, 128), F32), ((40, 128), F32),
            ((256, CELLS), BF16),
        ],
        [((96, 128), F32), ((512, 128), F32)],
    )
    (terms,) = run(
        functools.partial(
            step, 2.0 / flux_count, 2.0 / tensor_count, float(cell_count), breadth=breadth
        ),
        "step", [], [record, *weights],
        [((count, 16, 128), BF16)],
        [
            ((9 * BLOCK, CELLS), BF16), ((128, CELLS), BF16), ((640, CELLS), BF16),
            ((CELLS, CELLS), BF16), ((ROWS, 128), F32), ((count, 16, 128), F32),
        ],
    )
    terms = exchange(terms, ("y", "slab"))
    (routed,) = run(
        functools.partial(route, breadth=breadth), "route", [], [terms],
        [((depth, LAYERS, 128), BF16)], [((count, 16, 128), F32)],
    )
    routed = exchange(routed, "z")
    (share,) = run(spread, "spread", [], [routed], [((count, 4, 128), F32)])
    total = exchange(share, ("y", "slab"))
    fp, tp = run(
        place_records, "place", [], [routed], [((8, 3, 4, 64), BF16), ((8, 6), BF16)]
    )
    g1, b1, g2, b2, gs, gf, bf, gt, bt = run(
        finish, "finish", [], [total],
        [
            ((27, 1, 16), F32), ((1, 16), F32), ((432, 32), F32), ((1, 32), F32),
            ((16, 32), F32), ((3, 32), F32), ((1, 3), F32), ((6, 32), F32), ((1, 6), F32),
        ],
        [((ROWS, 128), F32), ((BLOCK, 32), F32)],
    )
    return (
        fp[:, :, None],
        tp,
        jnp.transpose(g1.reshape(3, 3, 3, 1, 16), (4, 3, 0, 1, 2)),
        b1.reshape(16),
        jnp.transpose(g2.reshape(3, 3, 3, 16, 32), (4, 3, 0, 1, 2)),
        b2.reshape(32),
        jnp.transpose(gs),
        gf,
        bf.reshape(3),
        gt,
        bt.reshape(6),
    )


def solution(mesh):
    breadth = 4
    grid = mesh.devices.reshape(-1, breadth, mesh.shape["slab"])
    mesh = jax.sharding.Mesh(grid, ("z", "y", "slab"))
    groups = ("z", "y")
    cells = P(groups, "slab", None, None)
    fields = P(groups, None, "slab", None, None)
    return jax.shard_map(
        on_device,
        mesh=mesh,
        in_specs=(cells, fields, P(groups, None), P(groups)) + (P(),) * 9,
        out_specs=(fields, P(groups, None)) + (P(),) * 9,
        check_vma=False,
    )
```

```python
import functools

import jax
import jax.numpy as jnp
from jax import lax
from jax.experimental import pallas as pl
from jax.experimental.pallas import tpu as pltpu
from jax.sharding import PartitionSpec as P

F32 = jnp.float32
BF16 = jnp.bfloat16
NN = (((1,), (0,)), ((), ()))
NT = (((1,), (1,)), ((), ()))
TN = (((0,), (0,)), ((), ()))

BLOCK = 144
CELLS = 512
TAPS = 144
ROWS = 128
SENT = 24
ROUTED = 40


def mxu(a, b, dims=NN):
    return lax.dot_general(a, b, dims, preferred_element_type=F32)


def lanes(shape):
    return lax.broadcasted_iota(jnp.int32, shape, len(shape) - 1)


def rows(shape):
    return lax.broadcasted_iota(jnp.int32, shape, len(shape) - 2)


def side_of(y):
    return ((y + 1) // 2) % 2


def pack(place_ref, vol_hbm, ft_hbm, out_ref, ft_ref, done):
    planes = pltpu.make_async_copy(vol_hbm, out_ref.at[:, 0:2], done.at[0])
    goals = pltpu.make_async_copy(ft_hbm, ft_ref, done.at[1])
    goals.start()
    planes.start()
    odd = place_ref[0] % 2 == 1
    goals.wait()
    goal = ft_ref[...].astype(F32)
    none = jnp.zeros_like(goal)
    low = jnp.concatenate([goal, none], axis=3)
    high = jnp.concatenate([none, goal], axis=3)
    both = jnp.where(odd, high, low)
    out_ref[:, 2] = jnp.concatenate([both[:, 0], both[:, 1]], axis=1).astype(BF16)
    rest = jnp.zeros((8, 4, 128), F32)
    out_ref[:, 3] = jnp.concatenate([both[:, 2], rest], axis=1).astype(BF16)
    planes.wait()


def prepare(
    place_ref, dest_ref, bf_ref,
    w1_ref, w2_ref, ws_ref, wf_ref, wt_ref, b1_ref, b2_ref, bt_ref, kt_ref,
    t1_ref, w2a_ref, wb_ref, wsb_ref, fw_ref, fwt_ref, cols_ref, wtt_ref, pick_ref,
    base, order,
):
    r, c = rows((256, CELLS)), lanes((256, CELLS))
    x = 2 * (c % 64) - 1 + c // 128
    pick = (r % 128 == x) & (r // 128 == (c % 128) // 64)
    pick_ref[...] = jnp.where(pick, 1.0, 0.0).astype(BF16)
    base[...] = jnp.zeros_like(base)
    for kz in range(3):
        for ky in range(3):
            for kx in range(3):
                at = kz * 32 + kx * 8 + ky
                base[at : at + 1, 0:16] = w1_ref[kz, ky, kx : kx + 1, :].astype(F32)
    taps = base[0:88]
    placed = jnp.zeros((128, 128), F32)
    for px in range(2):
        for z in range(2):
            down, right = z * 32 + px * 8, px * 32 + z * 16
            parts = [pltpu.roll(taps, right, 1) if right else taps]
            if down < 40:
                parts = parts + [jnp.zeros((40 - down, 128), F32)]
            if down:
                parts = [jnp.zeros((down, 128), F32)] + parts
            placed = placed + jnp.concatenate(parts, axis=0)
    across = jnp.transpose(placed)[0:64]
    place = lanes((64, 128)) % 8
    for y in range(8):
        own = across
        if y == 0:
            own = jnp.where(place == 0, 0.0, own)
        if y == 7:
            own = jnp.where(place == 2, 0.0, own)
        if y != 1:
            own = pltpu.roll(own, (y - 1) % 128, 1)
        t1_ref[y * 64 : y * 64 + 64, :] = own.astype(BF16)
    order[...] = jnp.zeros_like(order)
    w2 = w2_ref[...].astype(F32)
    for ky in range(3):
        for s, kx in enumerate((1, 2, 0)):
            for zo, kz in enumerate((1, 2, 0)):
                to, at = ky * 144 + s * 48 + zo * 16, ((kz * 3 + ky) * 3 + kx) * 16
                order[to : to + 16, 0:32] = w2[at : at + 16]
    order[432:448, 0:32] = ws_ref[...].astype(F32)
    w2t = order[...]
    w2a_ref[...] = jnp.transpose(w2t)[0:32].astype(BF16)
    wsb_ref[...] = w2t[432:448].astype(BF16)
    own, near = ((1, 0),), ((2, 0), (0, 1))
    for sub in range(2):
        for px in range(2):
            for z in range(2):
                sides = [jnp.zeros((16, 128), F32), jnp.zeros((16, 128), F32)]
                for ky, sy in near if sub else own:
                    for kx, sx in near if px else own:
                        for kz, sz in near if z else own:
                            at = ky * 144 + (1, 2, 0).index(kx) * 48 + (1, 2, 0).index(kz) * 16
                            to = sz * 64 + sx * 32
                            part = w2t[at : at + 16]
                            sides[sy] = sides[sy] + (pltpu.roll(part, to, 1) if to else part)
                to = sub * 64 + px * 32 + z * 16
                wb_ref[to : to + 16, :] = jnp.concatenate(sides, axis=1).astype(BF16)
    base[...] = jnp.zeros_like(base)
    base[0:3, 0:32] = wf_ref[...].astype(F32)
    wide = base[0:8, :]
    wide = wide + pltpu.roll(wide, 32, 1)
    wide = wide + pltpu.roll(wide, 64, 1)
    head = jnp.concatenate(
        [jnp.broadcast_to(wide[f : f + 1], (8, 128)) for f in range(3)]
        + [jnp.zeros((104, 128), F32)],
        axis=0,
    )
    mine = (lanes((128, 128)) // 32 == rows((128, 128)) % 8) & (rows((128, 128)) < 24)
    head = jnp.where(mine, head, 0.0)
    fw_ref[...] = head[0:32].astype(BF16)
    fwt_ref[...] = jnp.transpose(head).astype(BF16)
    base[...] = jnp.zeros_like(base)
    base[0:1, 0:16] = b1_ref[...]
    base[1:2, 0:32] = b2_ref[...]
    base[8:14, 0:32] = wt_ref[...].astype(F32)
    pad = jnp.zeros((120, 128), F32)
    cols_ref[...] = jnp.transpose(jnp.concatenate([base[0:8, :], pad], axis=0))
    wtt_ref[0:32] = jnp.transpose(jnp.concatenate([base[8:16, :], pad], axis=0))[0:32]
    base[16:24, 0:6] = kt_ref[...].astype(F32)
    wtt_ref[32:40] = jnp.zeros((8, 128), F32)
    wtt_ref[32:33, 0:6] = bt_ref[...]
    place = place_ref[0]
    mine = rows((8, 128)) == place
    wtt_ref[33:34] = jnp.sum(jnp.where(mine, base[16:24], 0.0), axis=0, keepdims=True)
    dest = dest_ref[place]
    group = jnp.maximum(dest, 0) // 8
    live = jnp.where(dest >= 0, 1.0, 0.0)
    wtt_ref[34:35] = jnp.broadcast_to(live, (1, 128))
    wtt_ref[35:36] = jnp.broadcast_to(dest.astype(F32), (1, 128))
    for t in range(2):
        leads = side_of(lax.axis_index("yh") * 2 + t) == side_of(group % 4)
        here = jnp.where((dest >= 0) & leads, 1.0, 0.0)
        wtt_ref[36 + t : 37 + t] = jnp.broadcast_to(here, (1, 128))
    rank = jnp.float32(0)
    for e in range(8):
        other = dest_ref[e]
        twin = (other >= 0) & (jnp.maximum(other, 0) // 8 == group) & (e < place)
        rank = jnp.where(twin, 1.0, rank)
    wtt_ref[38:39] = jnp.broadcast_to(rank, (1, 128))
    row = rows((128, 1))
    bias = jnp.where(row < 8, bf_ref[0], jnp.where(row < 16, bf_ref[1], bf_ref[2]))
    cols_ref[:, 2:3] = bias


def step(
    flux_scale, tensor_scale, cell_count,
    got_ref,
    t1_ref, w2a_ref, wb_ref, wsb_ref, fw_ref, fwt_ref, cols_ref, wtt_ref, pick_ref,
    out_ref,
    a_ref, a2_ref, d_ref, dz1_ref, total, extra, sent,
):
    live = wtt_ref[34:35, 0:1]
    empty = jnp.zeros((8, 128), F32)

    def plane(z):
        if z < 0 or z > 15:
            return empty
        return got_ref[z // 2, z % 2].astype(F32)

    low = jnp.concatenate([plane(4 * q - 1 + zi) for zi in range(4) for q in range(4)], axis=0)
    high = jnp.concatenate([plane(4 * q + 1 + zi) for zi in range(4) for q in range(4)], axis=0)
    cells = jnp.concatenate([low, high], axis=1).astype(BF16)
    apart = mxu(cells, pick_ref[...])
    lines = []
    for zi in range(4):
        for xt in range(4):
            lines.append(
                jnp.concatenate(
                    [
                        apart[zi * 32 + q * 8 : zi * 32 + q * 8 + 8, xt * 128 : xt * 128 + 128]
                        for q in range(4)
                    ],
                    axis=1,
                )
            )
    lines.append(jnp.where(rows((16, CELLS)) == 0, 1.0, 0.0))
    xcol = jnp.concatenate(lines, axis=0).astype(BF16)
    b1 = jnp.concatenate([cols_ref[0:16, 0:1]] * 4, axis=0)
    zero = jnp.zeros((), BF16)
    first_z = lanes((16, CELLS)) < 64
    first_x = lanes((48, CELLS)) % 64 == 0
    a_ref[0:BLOCK] = jnp.zeros((BLOCK, CELLS), BF16)
    z1_all = mxu(t1_ref[...], xcol[0:128])
    for y in range(8):
        z1 = z1_all[y * 64 : y * 64 + 64] + b1
        act = jnp.maximum(z1, 0.0).astype(BF16)
        at = (y + 1) * BLOCK
        for px in range(2):
            moved = pltpu.roll(act[px * 32 + 16 : px * 32 + 32], 64, 1)
            moved = jnp.where(first_z, zero, moved)
            a_ref[at + px * 48 : at + px * 48 + 32] = act[px * 32 : px * 32 + 32]
            a_ref[at + px * 48 + 32 : at + px * 48 + 48] = moved
        late = jnp.concatenate([act[32:64], moved], axis=0)
        a_ref[at + 96 : at + BLOCK] = jnp.where(first_x, zero, pltpu.roll(late, 1, 1))
    b2 = cols_ref[0:32, 1:2]
    pooled = jnp.zeros((32, 1), F32)
    for y in range(4):
        at = 2 * y * BLOCK
        z2 = mxu(w2a_ref[:, 0:432], a_ref[at : at + 432])
        short = mxu(w2a_ref[:, 432:448], a_ref[at + BLOCK : at + BLOCK + 16])
        z2 = (z2 + b2) + short
        act = jnp.maximum(z2, 0.0).astype(BF16)
        a2_ref[y * 32 : y * 32 + 32] = act
        pooled = pooled + jnp.sum(act.astype(F32), axis=1, keepdims=True)
    pooled = pooled / cell_count
    a2 = a2_ref[...]
    head = wtt_ref[0:32]
    tensor = jnp.sum(head * pooled, axis=0, keepdims=True) + wtt_ref[32:33]
    dt = tensor_scale * (tensor - wtt_ref[33:34]) * live
    spread = jnp.sum(head * dt, axis=1, keepdims=True) / cell_count
    row = rows((24, 1))
    full = mxu(fw_ref[0:24], a2) + cols_ref[0:24, 2:3]
    goals = [
        jnp.concatenate(
            [
                got_ref[2 * q, 2 + h].astype(F32) + got_ref[2 * q + 1, 2 + h].astype(F32)
                for q in range(4)
            ],
            axis=1,
        )
        for h in range(2)
    ]
    wanted = jnp.concatenate([goals[0], pltpu.roll(goals[0], 4, 0), goals[1]], axis=0)
    diff = flux_scale * (full - wanted) * live
    df = jnp.where(row % 8 < 4, diff, 0.0)
    df = jnp.concatenate([df, jnp.zeros((8, CELLS), F32)], axis=0).astype(BF16)
    member = lanes((8, CELLS)) // 64 == rows((8, CELLS))
    shares = []
    for f in range(3):
        for y in range(4):
            line = jnp.where(member, full[f * 8 + y : f * 8 + y + 1], 0.0)
            line = (line[:, 0:128] + line[:, 128:256]) + (line[:, 256:384] + line[:, 384:512])
            shares.append(line + pltpu.roll(line, 64, 1))
    left = lanes((8, 128)) < 64
    lane8 = lanes((8, 128))
    dest = wtt_ref[35:36]
    slot = dest - 8.0 * jnp.floor(dest / 8.0) + 1.0
    last = jnp.where(lane8 < 6, jnp.broadcast_to(tensor, (8, 128)), 0.0)
    last = jnp.where(lane8 == 6, dest, last)
    last = jnp.where(lane8 == 7, wtt_ref[38:39], last)
    last = jnp.where(lane8 == 8, slot, last)
    for t in range(2):
        here = wtt_ref[36 + t : 37 + t] > 0
        for k in range(6):
            both = jnp.where(left, shares[2 * k], shares[2 * k + 1])
            sent[t * 8 : t * 8 + 8, 16 + k, :] = jnp.where(here, both, 0.0)
        sent[t * 8 : t * 8 + 8, 22, :] = jnp.where(
            here, last, jnp.where(lane8 == 6, -1.0, 0.0)
        )
        sent[t * 8 : t * 8 + 8, 23, :] = jnp.zeros((8, 128), F32)
    last_x = lanes((32, CELLS)) % 64 == 63
    last_z = lanes((32, CELLS)) >= 448
    bias2 = jnp.zeros((32, 1), F32)
    dz2 = []
    for y in range(4):
        da2 = mxu(fwt_ref[y * 32 : y * 32 + 32, 0:32], df) + spread
        d = jnp.where(a2_ref[y * 32 : y * 32 + 32] > 0, da2, 0.0).astype(BF16)
        wide = d.astype(F32)
        bias2 = bias2 + jnp.sum(wide, axis=1, keepdims=True)
        next_x = jnp.where(last_x, zero, pltpu.roll(d, CELLS - 1, 1))
        next_z = jnp.where(last_z, zero, pltpu.roll(d, CELLS - 64, 1))
        both = jnp.where(last_z, zero, pltpu.roll(next_x, CELLS - 64, 1))
        d_ref[y * 128 : y * 128 + 32] = d
        d_ref[y * 128 + 32 : y * 128 + 64] = next_x
        d_ref[y * 128 + 64 : y * 128 + 96] = next_z
        d_ref[y * 128 + 96 : y * 128 + 128] = both
        dz2.append(d)
    d_ref[512:640] = jnp.zeros((128, CELLS), BF16)
    none = jnp.zeros((32, CELLS), BF16)
    second = jnp.zeros((BLOCK, 128), F32)
    for y in range(4):
        at = (2 * y + 1) * BLOCK
        da1 = mxu(wb_ref[...], d_ref[y * 128 : y * 128 + 256])
        short = mxu(wsb_ref[:, 0:32], dz2[y])
        da1 = jnp.concatenate([da1[0:16] + short, da1[16:128]], axis=0)
        for sub in range(2):
            act = a_ref[at + sub * BLOCK : at + sub * BLOCK + BLOCK]
            if sub == 0:
                sides = [none, dz2[y], none, none]
            else:
                sides = [dz2[y + 1] if y < 3 else none, none, dz2[y], none]
            second = second + mxu(act, jnp.concatenate(sides, axis=0), NT)
            on = jnp.concatenate([act[0:32], act[48:80]], axis=0) > 0
            dz1 = jnp.where(on, da1[sub * 64 : sub * 64 + 64], 0.0).astype(BF16)
            dz1_ref[(2 * y + sub) * 64 : (2 * y + sub) * 64 + 64] = dz1
    parts = mxu(dz1_ref[...], xcol, NT)
    place8 = lanes((64, 128)) % 8
    fold = jnp.zeros((64, 128), F32)
    tail = jnp.zeros((64, 1), F32)
    for y in range(8):
        part = parts[y * 64 : y * 64 + 64, 0:128]
        tail = tail + parts[y * 64 : y * 64 + 64, 128:129]
        if y == 0:
            part = jnp.where(place8 == 7, 0.0, part)
        if y == 7:
            part = jnp.where(place8 == 0, 0.0, part)
        if y != 1:
            part = pltpu.roll(part, (1 - y) % 128, 1)
        fold = fold + part
    first = jnp.zeros((16, 128), F32)
    first_bias = jnp.zeros((16, 1), F32)
    for px in range(2):
        for z in range(2):
            at, left = px * 32 + z * 16, z * 32 + px * 8
            part = fold[at : at + 16]
            first = first + (pltpu.roll(part, 128 - left, 1) if left else part)
            first_bias = first_bias + tail[at : at + 16]
    lane = lanes((1, 128))
    bias2 = jnp.where(lanes((32, 128)) == 0, bias2, pooled * pltpu.roll(dt, 1, 1))
    upright = jnp.concatenate(
        [
            jnp.where(lanes((16, 128)) == 127, first_bias, first),
            jnp.zeros((16, 128), F32),
            bias2,
            jnp.zeros((64, 128), F32),
        ],
        axis=0,
    )
    upright = jnp.transpose(upright)
    cross = mxu(df, a2, NT)
    same = lanes((32, 128)) // 32 == rows((32, 128)) % 8
    cross = jnp.where(same, cross, 0.0)
    cross = cross + pltpu.roll(cross, 64, 1)
    cross = cross + pltpu.roll(cross, 32, 1)
    flux_sum = jnp.sum(df.astype(F32), axis=1, keepdims=True)
    for ky in range(3):
        tail_block = pltpu.roll(second[128:144], (96 - ky * 32) % 128, 1)
        extra[ky * 16 : ky * 16 + 16] = tail_block
    lane8 = lanes((8, 128))
    for i in range(5):
        pair = jnp.zeros((8, 128), F32)
        for h in range(2 if i < 4 else 1):
            g = 2 * i + h
            at = (g // 3) * 32 + (g % 3) * 8
            part = jnp.where(lane8 < 16, upright[at : at + 8], 0.0)
            pair = pair + pltpu.roll(part, 96 + 16 * h, 1)
        extra[48 + 3 * i : 51 + 3 * i] = pair[0:3]
    bias_row = jnp.zeros((1, 128), F32)
    for f in range(3):
        extra[63 + f : 64 + f] = jnp.sum(cross[f * 8 : f * 8 + 8], axis=0, keepdims=True)
        sums = jnp.sum(flux_sum[f * 8 : f * 8 + 8], axis=0, keepdims=True)
        bias_row = jnp.where(lane == 112 + f, sums, bias_row)
    extra[66:67] = pltpu.roll(upright[0:1], 64, 1)
    first_row = pltpu.roll(jnp.where(lane < 16, upright[127:128], 0.0), 96, 1)
    tensor_row = pltpu.roll(jnp.where(lane < 6, dt, 0.0), 116, 1)
    extra[67:68] = first_row + bias_row + tensor_row
    extra[68:74] = pltpu.roll(upright[0:8], 64, 1)[1:7]
    extra[74:112] = jnp.zeros((38, 128), F32)
    rest = lane8 >= 96
    swap = lax.axis_index("yh") * 8
    for t in range(16):
        block = second[t * 8 : t * 8 + 8]
        total[t * 8 : t * 8 + 8] = jnp.where(rest, 0.0, block)
        total[t * 8 : t * 8 + 7] = jnp.where(
            rest[0:7], extra[t * 7 : t * 7 + 7], block[0:7]
        )
        block = total[t * 8 : t * 8 + 8]
        high = block.astype(BF16).astype(F32)
        to = lax.rem(t + swap, 16)
        sent[to, 0:8, :] = high
        sent[to, 8:16, :] = block - high
    out_ref[...] = sent[...].astype(BF16)


def route(got_ref, out_ref, recs):
    recs[...] = got_ref[...].astype(F32)
    count = got_ref.shape[0]
    full = recs[0, 0:8, :] + recs[0, 8:16, :]
    for p in range(1, count):
        full = full + (recs[p, 0:8, :] + recs[p, 8:16, :])
    high = full.astype(BF16).astype(F32)
    low = full - high
    peers = out_ref.shape[0]
    lane = lanes((count, 128))
    last = recs[:, 22, :]
    dest = jnp.sum(jnp.where(lane == 6, last, 0.0), axis=1, keepdims=True).astype(jnp.int32)
    rank = jnp.sum(jnp.where(lane == 7, last, 0.0), axis=1, keepdims=True).astype(jnp.int32)
    side = side_of(lax.axis_index("yh") * 2 + lax.axis_index("yl"))
    peer = lane // 4
    group = (peer // 2) * 4 + jnp.where(peer % 2 == 0, side, 3 - side)
    seat = (rows((count, 128)) // 8) * 2 + rank
    right = (dest >= group * 8) & (dest < group * 8 + 8) & (seat == lane % 4)
    hit = jnp.where(right & (peer < peers), 1.0, 0.0)
    hit = jnp.concatenate([hit, jnp.zeros((128 - count, 128), F32)], axis=0)
    choose = jnp.transpose(hit)[0 : 4 * peers, 0:count].astype(BF16)
    layers = [mxu(choose, recs[:, 16 + k, :].astype(BF16)) for k in range(6)]
    marks = mxu(choose, last.astype(BF16))
    marks = jnp.where(lanes((4 * peers, 128)) < 16, marks, 0.0)
    marks = [pltpu.roll(marks, 96, 1), pltpu.roll(marks, 112, 1)]
    row8, lane8 = rows((8, 128)), lanes((8, 128))
    upper, spare = row8 < 4, (row8 == 7) & (lane8 >= 96)
    for i in range(peers):
        tall = []
        for h, part in enumerate((high, low)):
            at = 4 * i + 2 * h
            seats = marks[0][at : at + 1] + marks[1][at + 1 : at + 2]
            tall.append(jnp.where(spare, seats, part))
        at = (i // 2) * 8
        for m in range(3):
            even, odd = layers[2 * m][at : at + 8], layers[2 * m + 1][at : at + 8]
            if i % 2 == 0:
                tall.append(jnp.where(upper, even, pltpu.roll(odd, 4, 0)))
            else:
                tall.append(jnp.where(upper, pltpu.roll(even, 4, 0), odd))
        out_ref[i] = jnp.concatenate(tall, axis=0).astype(BF16)


def spread(got_ref, out_ref):
    parts = jnp.sum(got_ref[:, 0:16, :].astype(F32), axis=0)
    share = parts[0:8] + parts[8:16]
    out_ref[...] = jnp.broadcast_to(share[None], out_ref.shape)


def place_records(got_ref, fp_ref, tp_ref, recs):
    recs[...] = got_ref[...].astype(F32)
    count = got_ref.shape[0]
    marks = [
        pltpu.roll(recs[:, 7 + 8 * (j // 2), :], 32 - 16 * (j % 2), 1) for j in range(4)
    ]
    marks = jnp.concatenate(marks, axis=0)
    lane = lanes((4 * count, 128))
    slot = jnp.sum(jnp.where(lane == 8, marks, 0.0), axis=1, keepdims=True) - 1.0
    hit = jnp.where((slot == lane.astype(F32)) & (lane < 8), 1.0, 0.0)
    hit = jnp.concatenate([hit, jnp.zeros((128 - 4 * count, 128), F32)], axis=0)
    choose = jnp.transpose(hit)[0:8, 0 : 4 * count].astype(BF16)
    for k in range(6):
        held = jnp.concatenate([recs[:, 16 + 4 * k + j, :] for j in range(4)], axis=0)
        got = mxu(choose, held.astype(BF16)).astype(BF16)
        f, y = (2 * k) // 4, (2 * k) % 4
        fp_ref[:, f, y, :] = got[:, 0:64]
        fp_ref[:, f, y + 1, :] = got[:, 64:128]
    tp_ref[...] = mxu(choose, marks.astype(BF16))[:, 0:6].astype(BF16)


def finish(
    got_ref,
    g1_ref, b1_ref, g2_ref, b2_ref, gs_ref, gf_ref, bf_ref, gt_ref, bt_ref,
    total, extra, second,
):
    swap = lax.axis_index("yh") * 8
    for p in range(16):
        block = got_ref[lax.rem(p + swap, 16)]
        total[p * 8 : p * 8 + 8] = block
        extra[p * 7 : p * 7 + 7] = block[0:7, 96:128]
    for kz in range(3):
        for ky in range(3):
            for kx in range(3):
                g = kz * 3 + kx
                at, to = 48 + 3 * (g // 2) + ky, 16 * (g % 2)
                g1_ref[(kz * 3 + ky) * 3 + kx] = extra[at : at + 1, to : to + 16]
    for ky in range(3):
        second[0:128] = total[0:128, ky * 32 : ky * 32 + 32]
        second[128:144] = extra[ky * 16 : ky * 16 + 16]
        for s, kx in enumerate((1, 2, 0)):
            for zo, kz in enumerate((1, 2, 0)):
                to = ((kz * 3 + ky) * 3 + kx) * 16
                part = second[s * 48 + zo * 16 : s * 48 + zo * 16 + 16]
                g2_ref[to : to + 16] = part
                if ky == 1 and kx == 1 and kz == 1:
                    gs_ref[...] = part
    gf_ref[...] = extra[63:66]
    b2_ref[...] = extra[66:67]
    b1_ref[...] = extra[67:68, 0:16]
    bf_ref[...] = extra[67:68, 16:19]
    bt_ref[...] = extra[67:68, 20:26]
    gt_ref[...] = extra[68:74]


SMEM = pl.BlockSpec(memory_space=pltpu.SMEM)
VMEM = pl.BlockSpec(memory_space=pltpu.VMEM)
MIB = 1024 * 1024


def run(kernel, name, scalars, arrays, outs, scratch=(), held=None, limit=16):
    return pl.pallas_call(
        kernel,
        out_shape=tuple(jax.ShapeDtypeStruct(*o[0:2]) for o in outs),
        in_specs=[SMEM] * len(scalars) + [held or VMEM] * len(arrays),
        out_specs=tuple(o[2] if len(o) > 2 else VMEM for o in outs),
        scratch_shapes=[pltpu.VMEM(*s) if isinstance(s, tuple) else s for s in scratch],
        compiler_params=pltpu.CompilerParams(vmem_limit_bytes=limit * MIB),
        name=name,
    )(*scalars, *arrays)


def exchange(block, axis, groups=None):
    return lax.all_to_all(block, axis, 0, 0, tiled=True, axis_index_groups=groups)


def on_device(
    volume, flux_target, tensor_target, dest,
    first_weight, first_bias, second_weight, second_bias, short_weight,
    flux_weight, flux_bias, tensor_weight, tensor_bias,
):
    depth, slabs = lax.axis_size("z"), lax.axis_size("slab")
    near, far = 2 * slabs, 2 * depth
    lines = [[z * 4 + y for z in range(depth) for y in pair] for pair in ((0, 3), (1, 2))]
    records = 8 * depth * 4
    flux_count = records * 3 * slabs * 4 * 64
    tensor_count = records * 6
    cell_count = slabs * 4 * 64
    place = lax.axis_index("slab").astype(jnp.int32).reshape(1)
    (mine,) = run(
        pack, "pack", [place], [volume, flux_target[:, :, 0]], [((8, 4, 8, 128), BF16)],
        [((8, 3, 4, 64), BF16), pltpu.SemaphoreType.DMA((2,))],
        pl.BlockSpec(memory_space=pl.ANY), 60,
    )
    record = exchange(mine, "slab")
    weights = run(
        prepare, "prepare", [place, dest, flux_bias],
        [
            jnp.transpose(first_weight[:, 0], (1, 2, 3, 0)),
            jnp.transpose(second_weight, (2, 3, 4, 1, 0)).reshape(432, 32),
            jnp.transpose(short_weight),
            flux_weight, tensor_weight,
            first_bias.reshape(1, 16), second_bias.reshape(1, 32), tensor_bias.reshape(1, 6),
            tensor_target,
        ],
        [
            ((512, 128), BF16), ((32, 512), BF16), ((128, 256), BF16), ((16, 128), BF16),
            ((32, 128), BF16), ((128, 128), BF16), ((128, 128), F32), ((40, 128), F32),
            ((256, CELLS), BF16),
        ],
        [((96, 128), F32), ((512, 128), F32)],
    )
    (terms,) = run(
        functools.partial(step, 2.0 / flux_count, 2.0 / tensor_count, float(cell_count)),
        "step", [], [record, *weights], [((near, SENT, 128), BF16)],
        [
            ((9 * BLOCK, CELLS), BF16), ((128, CELLS), BF16), ((640, CELLS), BF16),
            ((CELLS, CELLS), BF16), ((ROWS, 128), F32), ((112, 128), F32),
            ((near, SENT, 128), F32),
        ],
    )
    terms = exchange(terms, ("yl", "slab"))
    (routed,) = run(
        route, "route", [], [terms], [((far, ROUTED, 128), BF16)],
        [((near, SENT, 128), F32)],
    )
    routed = exchange(routed, ("z", "yh", "yl"), lines)
    (share,) = run(spread, "spread", [], [routed], [((near, 8, 128), F32)])
    total = exchange(share, ("yl", "slab"))
    fp, tp = run(
        place_records, "place", [], [routed], [((8, 3, 4, 64), BF16), ((8, 6), BF16)],
        [((far, ROUTED, 128), F32)],
    )
    g1, b1, g2, b2, gs, gf, bf, gt, bt = run(
        finish, "finish", [], [total],
        [
            ((27, 1, 16), F32), ((1, 16), F32), ((432, 32), F32), ((1, 32), F32),
            ((16, 32), F32), ((3, 32), F32), ((1, 3), F32), ((6, 32), F32), ((1, 6), F32),
        ],
        [((ROWS, 128), F32), ((112, 32), F32), ((BLOCK, 32), F32)],
    )
    return (
        fp[:, :, None],
        tp,
        jnp.transpose(g1.reshape(3, 3, 3, 1, 16), (4, 3, 0, 1, 2)),
        b1.reshape(16),
        jnp.transpose(g2.reshape(3, 3, 3, 16, 32), (4, 3, 0, 1, 2)),
        b2.reshape(32),
        jnp.transpose(gs),
        gf,
        bf.reshape(3),
        gt,
        bt.reshape(6),
    )


def solution(mesh):
    grid = mesh.devices.reshape(-1, 2, 2, mesh.shape["slab"])
    mesh = jax.sharding.Mesh(grid, ("z", "yh", "yl", "slab"))
    groups = ("z", "yh", "yl")
    cells = P(groups, "slab", None, None)
    fields = P(groups, None, "slab", None, None)
    return jax.shard_map(
        on_device,
        mesh=mesh,
        in_specs=(cells, fields, P(groups, None), P(groups)) + (P(),) * 9,
        out_specs=(fields, P(groups, None)) + (P(),) * 9,
        check_vma=False,
    )
```

```python
import functools

import jax
import jax.numpy as jnp
from jax import lax
from jax.experimental import pallas as pl
from jax.experimental.pallas import tpu as pltpu
from jax.sharding import PartitionSpec as P

F32 = jnp.float32
BF16 = jnp.bfloat16
NN = (((1,), (0,)), ((), ()))
NT = (((1,), (1,)), ((), ()))
TN = (((0,), (0,)), ((), ()))

BLOCK = 144
CELLS = 512
TAPS = 144
ROWS = 128
SENT = 24
ROUTED = 40


def mxu(a, b, dims=NN):
    return lax.dot_general(a, b, dims, preferred_element_type=F32)


def lanes(shape):
    return lax.broadcasted_iota(jnp.int32, shape, len(shape) - 1)


def rows(shape):
    return lax.broadcasted_iota(jnp.int32, shape, len(shape) - 2)


def side_of(y):
    return ((y + 1) // 2) % 2


def prepare(
    place_ref, dest_ref, bf_ref,
    w1_ref, w2_ref, ws_ref, wf_ref, wt_ref, b1_ref, b2_ref, bt_ref, kt_ref,
    t1_ref, w2a_ref, wb_ref, wsb_ref, fw_ref, fwt_ref, cols_ref, wtt_ref, pick_ref,
    base, order,
):
    r, c = rows((256, CELLS)), lanes((256, CELLS))
    x = 2 * (c % 64) - 1 + c // 128
    pick = (r % 128 == x) & (r // 128 == (c % 128) // 64)
    pick_ref[...] = jnp.where(pick, 1.0, 0.0).astype(BF16)
    base[...] = jnp.zeros_like(base)
    for kz in range(3):
        for ky in range(3):
            for kx in range(3):
                at = kz * 32 + kx * 8 + ky
                base[at : at + 1, 0:16] = w1_ref[kz, ky, kx : kx + 1, :].astype(F32)
    taps = base[0:88]
    placed = jnp.zeros((128, 128), F32)
    for px in range(2):
        for z in range(2):
            down, right = z * 32 + px * 8, px * 32 + z * 16
            parts = [pltpu.roll(taps, right, 1) if right else taps]
            if down < 40:
                parts = parts + [jnp.zeros((40 - down, 128), F32)]
            if down:
                parts = [jnp.zeros((down, 128), F32)] + parts
            placed = placed + jnp.concatenate(parts, axis=0)
    across = jnp.transpose(placed)[0:64]
    place = lanes((64, 128)) % 8
    for y in range(8):
        own = across
        if y == 0:
            own = jnp.where(place == 0, 0.0, own)
        if y == 7:
            own = jnp.where(place == 2, 0.0, own)
        if y != 1:
            own = pltpu.roll(own, (y - 1) % 128, 1)
        t1_ref[y * 64 : y * 64 + 64, :] = own.astype(BF16)
    order[...] = jnp.zeros_like(order)
    w2 = w2_ref[...].astype(F32)
    for ky in range(3):
        for s, kx in enumerate((1, 2, 0)):
            for zo, kz in enumerate((1, 2, 0)):
                to, at = ky * 144 + s * 48 + zo * 16, ((kz * 3 + ky) * 3 + kx) * 16
                order[to : to + 16, 0:32] = w2[at : at + 16]
    order[432:448, 0:32] = ws_ref[...].astype(F32)
    w2t = order[...]
    w2a_ref[...] = jnp.transpose(w2t)[0:32].astype(BF16)
    wsb_ref[...] = w2t[432:448].astype(BF16)
    own, near = ((1, 0),), ((2, 0), (0, 1))
    for sub in range(2):
        for px in range(2):
            for z in range(2):
                sides = [jnp.zeros((16, 128), F32), jnp.zeros((16, 128), F32)]
                for ky, sy in near if sub else own:
                    for kx, sx in near if px else own:
                        for kz, sz in near if z else own:
                            at = ky * 144 + (1, 2, 0).index(kx) * 48 + (1, 2, 0).index(kz) * 16
                            to = sz * 64 + sx * 32
                            part = w2t[at : at + 16]
                            sides[sy] = sides[sy] + (pltpu.roll(part, to, 1) if to else part)
                to = sub * 64 + px * 32 + z * 16
                wb_ref[to : to + 16, :] = jnp.concatenate(sides, axis=1).astype(BF16)
    base[...] = jnp.zeros_like(base)
    base[0:3, 0:32] = wf_ref[...].astype(F32)
    wide = base[0:8, :]
    wide = wide + pltpu.roll(wide, 32, 1)
    wide = wide + pltpu.roll(wide, 64, 1)
    head = jnp.concatenate(
        [jnp.broadcast_to(wide[f : f + 1], (8, 128)) for f in range(3)]
        + [jnp.zeros((104, 128), F32)],
        axis=0,
    )
    mine = (lanes((128, 128)) // 32 == rows((128, 128)) % 8) & (rows((128, 128)) < 24)
    head = jnp.where(mine, head, 0.0)
    fw_ref[...] = head[0:32].astype(BF16)
    fwt_ref[...] = jnp.transpose(head).astype(BF16)
    base[...] = jnp.zeros_like(base)
    base[0:1, 0:16] = b1_ref[...]
    base[1:2, 0:32] = b2_ref[...]
    base[8:14, 0:32] = wt_ref[...].astype(F32)
    pad = jnp.zeros((120, 128), F32)
    cols_ref[...] = jnp.transpose(jnp.concatenate([base[0:8, :], pad], axis=0))
    wtt_ref[0:32] = jnp.transpose(jnp.concatenate([base[8:16, :], pad], axis=0))[0:32]
    base[16:24, 0:6] = kt_ref[...].astype(F32)
    wtt_ref[32:40] = jnp.zeros((8, 128), F32)
    wtt_ref[32:33, 0:6] = bt_ref[...]
    place = place_ref[0]
    mine = rows((8, 128)) == place
    wtt_ref[33:34] = jnp.sum(jnp.where(mine, base[16:24], 0.0), axis=0, keepdims=True)
    dest = dest_ref[place]
    group = jnp.maximum(dest, 0) // 8
    live = jnp.where(dest >= 0, 1.0, 0.0)
    wtt_ref[34:35] = jnp.broadcast_to(live, (1, 128))
    wtt_ref[35:36] = jnp.broadcast_to(dest.astype(F32), (1, 128))
    for t in range(2):
        leads = side_of(lax.axis_index("yh") * 2 + t) == side_of(group % 4)
        here = jnp.where((dest >= 0) & leads, 1.0, 0.0)
        wtt_ref[36 + t : 37 + t] = jnp.broadcast_to(here, (1, 128))
    rank = jnp.float32(0)
    for e in range(8):
        other = dest_ref[e]
        twin = (other >= 0) & (jnp.maximum(other, 0) // 8 == group) & (e < place)
        rank = jnp.where(twin, 1.0, rank)
    wtt_ref[38:39] = jnp.broadcast_to(rank, (1, 128))
    row = rows((128, 1))
    bias = jnp.where(row < 8, bf_ref[0], jnp.where(row < 16, bf_ref[1], bf_ref[2]))
    cols_ref[:, 2:3] = bias


def step(
    flux_scale, tensor_scale, cell_count,
    got_ref,
    t1_ref, w2a_ref, wb_ref, wsb_ref, fw_ref, fwt_ref, cols_ref, wtt_ref, pick_ref,
    out_ref,
    a_ref, a2_ref, d_ref, dz1_ref, total, extra, sent,
):
    live = wtt_ref[34:35, 0:1]
    empty = jnp.zeros((8, 128), F32)

    def plane(z):
        if z < 0 or z > 15:
            return empty
        return got_ref[z // 2, z % 2].astype(F32)

    low = jnp.concatenate([plane(4 * q - 1 + zi) for zi in range(4) for q in range(4)], axis=0)
    high = jnp.concatenate([plane(4 * q + 1 + zi) for zi in range(4) for q in range(4)], axis=0)
    cells = jnp.concatenate([low, high], axis=1).astype(BF16)
    apart = mxu(cells, pick_ref[...])
    lines = []
    for zi in range(4):
        for xt in range(4):
            lines.append(
                jnp.concatenate(
                    [
                        apart[zi * 32 + q * 8 : zi * 32 + q * 8 + 8, xt * 128 : xt * 128 + 128]
                        for q in range(4)
                    ],
                    axis=1,
                )
            )
    lines.append(jnp.where(rows((16, CELLS)) == 0, 1.0, 0.0))
    xcol = jnp.concatenate(lines, axis=0).astype(BF16)
    b1 = jnp.concatenate([cols_ref[0:16, 0:1]] * 4, axis=0)
    zero = jnp.zeros((), BF16)
    first_z = lanes((16, CELLS)) < 64
    first_x = lanes((48, CELLS)) % 64 == 0
    a_ref[0:BLOCK] = jnp.zeros((BLOCK, CELLS), BF16)
    z1_all = mxu(t1_ref[...], xcol[0:128])
    for y in range(8):
        z1 = z1_all[y * 64 : y * 64 + 64] + b1
        act = jnp.maximum(z1, 0.0).astype(BF16)
        at = (y + 1) * BLOCK
        for px in range(2):
            moved = pltpu.roll(act[px * 32 + 16 : px * 32 + 32], 64, 1)
            moved = jnp.where(first_z, zero, moved)
            a_ref[at + px * 48 : at + px * 48 + 32] = act[px * 32 : px * 32 + 32]
            a_ref[at + px * 48 + 32 : at + px * 48 + 48] = moved
        late = jnp.concatenate([act[32:64], moved], axis=0)
        a_ref[at + 96 : at + BLOCK] = jnp.where(first_x, zero, pltpu.roll(late, 1, 1))
    b2 = cols_ref[0:32, 1:2]
    pooled = jnp.zeros((32, 1), F32)
    for y in range(4):
        at = 2 * y * BLOCK
        z2 = mxu(w2a_ref[:, 0:432], a_ref[at : at + 432])
        short = mxu(w2a_ref[:, 432:448], a_ref[at + BLOCK : at + BLOCK + 16])
        z2 = (z2 + b2) + short
        act = jnp.maximum(z2, 0.0).astype(BF16)
        a2_ref[y * 32 : y * 32 + 32] = act
        pooled = pooled + jnp.sum(act.astype(F32), axis=1, keepdims=True)
    pooled = pooled / cell_count
    a2 = a2_ref[...]
    head = wtt_ref[0:32]
    tensor = jnp.sum(head * pooled, axis=0, keepdims=True) + wtt_ref[32:33]
    dt = tensor_scale * (tensor - wtt_ref[33:34]) * live
    spread = jnp.sum(head * dt, axis=1, keepdims=True) / cell_count
    row = rows((24, 1))
    full = mxu(fw_ref[0:24], a2) + cols_ref[0:24, 2:3]
    goals = [
        jnp.concatenate(
            [
                got_ref[2 * q, 2 + h].astype(F32)
                + pltpu.roll(got_ref[2 * q + 1, 2 + h].astype(F32), 64, 1)
                for q in range(4)
            ],
            axis=1,
        )
        for h in range(2)
    ]
    wanted = jnp.concatenate([goals[0], pltpu.roll(goals[0], 4, 0), goals[1]], axis=0)
    diff = flux_scale * (full - wanted) * live
    df = jnp.where(row % 8 < 4, diff, 0.0)
    df = jnp.concatenate([df, jnp.zeros((8, CELLS), F32)], axis=0).astype(BF16)
    member = lanes((8, CELLS)) // 64 == rows((8, CELLS))
    shares = []
    for f in range(3):
        for y in range(4):
            line = jnp.where(member, full[f * 8 + y : f * 8 + y + 1], 0.0)
            line = (line[:, 0:128] + line[:, 128:256]) + (line[:, 256:384] + line[:, 384:512])
            shares.append(line + pltpu.roll(line, 64, 1))
    left = lanes((8, 128)) < 64
    lane8 = lanes((8, 128))
    dest = wtt_ref[35:36]
    slot = dest - 8.0 * jnp.floor(dest / 8.0) + 1.0
    last = jnp.where(lane8 < 6, jnp.broadcast_to(tensor, (8, 128)), 0.0)
    last = jnp.where(lane8 == 6, dest, last)
    last = jnp.where(lane8 == 7, wtt_ref[38:39], last)
    last = jnp.where(lane8 == 8, slot, last)
    for t in range(2):
        here = wtt_ref[36 + t : 37 + t] > 0
        for k in range(6):
            both = jnp.where(left, shares[2 * k], shares[2 * k + 1])
            sent[t * 8 : t * 8 + 8, 16 + k, :] = jnp.where(here, both, 0.0)
        sent[t * 8 : t * 8 + 8, 22, :] = jnp.where(
            here, last, jnp.where(lane8 == 6, -1.0, 0.0)
        )
        sent[t * 8 : t * 8 + 8, 23, :] = jnp.zeros((8, 128), F32)
    last_x = lanes((32, CELLS)) % 64 == 63
    last_z = lanes((32, CELLS)) >= 448
    bias2 = jnp.zeros((32, 1), F32)
    dz2 = []
    for y in range(4):
        da2 = mxu(fwt_ref[y * 32 : y * 32 + 32, 0:32], df) + spread
        d = jnp.where(a2_ref[y * 32 : y * 32 + 32] > 0, da2, 0.0).astype(BF16)
        wide = d.astype(F32)
        bias2 = bias2 + jnp.sum(wide, axis=1, keepdims=True)
        next_x = jnp.where(last_x, zero, pltpu.roll(d, CELLS - 1, 1))
        next_z = jnp.where(last_z, zero, pltpu.roll(d, CELLS - 64, 1))
        both = jnp.where(last_z, zero, pltpu.roll(next_x, CELLS - 64, 1))
        d_ref[y * 128 : y * 128 + 32] = d
        d_ref[y * 128 + 32 : y * 128 + 64] = next_x
        d_ref[y * 128 + 64 : y * 128 + 96] = next_z
        d_ref[y * 128 + 96 : y * 128 + 128] = both
        dz2.append(d)
    d_ref[512:640] = jnp.zeros((128, CELLS), BF16)
    none = jnp.zeros((32, CELLS), BF16)
    second = jnp.zeros((BLOCK, 128), F32)
    for y in range(4):
        at = (2 * y + 1) * BLOCK
        da1 = mxu(wb_ref[...], d_ref[y * 128 : y * 128 + 256])
        short = mxu(wsb_ref[:, 0:32], dz2[y])
        da1 = jnp.concatenate([da1[0:16] + short, da1[16:128]], axis=0)
        for sub in range(2):
            act = a_ref[at + sub * BLOCK : at + sub * BLOCK + BLOCK]
            if sub == 0:
                sides = [none, dz2[y], none, none]
            else:
                sides = [dz2[y + 1] if y < 3 else none, none, dz2[y], none]
            second = second + mxu(act, jnp.concatenate(sides, axis=0), NT)
            on = jnp.concatenate([act[0:32], act[48:80]], axis=0) > 0
            dz1 = jnp.where(on, da1[sub * 64 : sub * 64 + 64], 0.0).astype(BF16)
            dz1_ref[(2 * y + sub) * 64 : (2 * y + sub) * 64 + 64] = dz1
    parts = mxu(dz1_ref[...], xcol, NT)
    place8 = lanes((64, 128)) % 8
    fold = jnp.zeros((64, 128), F32)
    tail = jnp.zeros((64, 1), F32)
    for y in range(8):
        part = parts[y * 64 : y * 64 + 64, 0:128]
        tail = tail + parts[y * 64 : y * 64 + 64, 128:129]
        if y == 0:
            part = jnp.where(place8 == 7, 0.0, part)
        if y == 7:
            part = jnp.where(place8 == 0, 0.0, part)
        if y != 1:
            part = pltpu.roll(part, (1 - y) % 128, 1)
        fold = fold + part
    first = jnp.zeros((16, 128), F32)
    first_bias = jnp.zeros((16, 1), F32)
    for px in range(2):
        for z in range(2):
            at, left = px * 32 + z * 16, z * 32 + px * 8
            part = fold[at : at + 16]
            first = first + (pltpu.roll(part, 128 - left, 1) if left else part)
            first_bias = first_bias + tail[at : at + 16]
    lane = lanes((1, 128))
    bias2 = jnp.where(lanes((32, 128)) == 0, bias2, pooled * pltpu.roll(dt, 1, 1))
    upright = jnp.concatenate(
        [
            jnp.where(lanes((16, 128)) == 127, first_bias, first),
            jnp.zeros((16, 128), F32),
            bias2,
            jnp.zeros((64, 128), F32),
        ],
        axis=0,
    )
    upright = jnp.transpose(upright)
    cross = mxu(df, a2, NT)
    same = lanes((32, 128)) // 32 == rows((32, 128)) % 8
    cross = jnp.where(same, cross, 0.0)
    cross = cross + pltpu.roll(cross, 64, 1)
    cross = cross + pltpu.roll(cross, 32, 1)
    flux_sum = jnp.sum(df.astype(F32), axis=1, keepdims=True)
    for ky in range(3):
        tail_block = pltpu.roll(second[128:144], (96 - ky * 32) % 128, 1)
        extra[ky * 16 : ky * 16 + 16] = tail_block
    lane8 = lanes((8, 128))
    for i in range(5):
        pair = jnp.zeros((8, 128), F32)
        for h in range(2 if i < 4 else 1):
            g = 2 * i + h
            at = (g // 3) * 32 + (g % 3) * 8
            part = jnp.where(lane8 < 16, upright[at : at + 8], 0.0)
            pair = pair + pltpu.roll(part, 96 + 16 * h, 1)
        extra[48 + 3 * i : 51 + 3 * i] = pair[0:3]
    bias_row = jnp.zeros((1, 128), F32)
    for f in range(3):
        extra[63 + f : 64 + f] = jnp.sum(cross[f * 8 : f * 8 + 8], axis=0, keepdims=True)
        sums = jnp.sum(flux_sum[f * 8 : f * 8 + 8], axis=0, keepdims=True)
        bias_row = jnp.where(lane == 112 + f, sums, bias_row)
    extra[66:67] = pltpu.roll(upright[0:1], 64, 1)
    first_row = pltpu.roll(jnp.where(lane < 16, upright[127:128], 0.0), 96, 1)
    tensor_row = pltpu.roll(jnp.where(lane < 6, dt, 0.0), 116, 1)
    extra[67:68] = first_row + bias_row + tensor_row
    extra[68:74] = pltpu.roll(upright[0:8], 64, 1)[1:7]
    extra[74:112] = jnp.zeros((38, 128), F32)
    rest = lane8 >= 96
    swap = lax.axis_index("yh") * 8
    for t in range(16):
        block = second[t * 8 : t * 8 + 8]
        total[t * 8 : t * 8 + 8] = jnp.where(rest, 0.0, block)
        total[t * 8 : t * 8 + 7] = jnp.where(
            rest[0:7], extra[t * 7 : t * 7 + 7], block[0:7]
        )
        block = total[t * 8 : t * 8 + 8]
        high = block.astype(BF16).astype(F32)
        to = lax.rem(t + swap, 16)
        sent[to, 0:8, :] = high
        sent[to, 8:16, :] = block - high
    out_ref[...] = sent[...].astype(BF16)


def route(got_ref, out_ref, recs):
    recs[...] = got_ref[...].astype(F32)
    count = got_ref.shape[0]
    full = recs[0, 0:8, :] + recs[0, 8:16, :]
    for p in range(1, count):
        full = full + (recs[p, 0:8, :] + recs[p, 8:16, :])
    high = full.astype(BF16).astype(F32)
    low = full - high
    peers = out_ref.shape[0]
    lane = lanes((count, 128))
    last = recs[:, 22, :]
    dest = jnp.sum(jnp.where(lane == 6, last, 0.0), axis=1, keepdims=True).astype(jnp.int32)
    rank = jnp.sum(jnp.where(lane == 7, last, 0.0), axis=1, keepdims=True).astype(jnp.int32)
    side = side_of(lax.axis_index("yh") * 2 + lax.axis_index("yl"))
    peer = lane // 4
    group = (peer // 2) * 4 + jnp.where(peer % 2 == 0, side, 3 - side)
    seat = (rows((count, 128)) // 8) * 2 + rank
    right = (dest >= group * 8) & (dest < group * 8 + 8) & (seat == lane % 4)
    hit = jnp.where(right & (peer < peers), 1.0, 0.0)
    hit = jnp.concatenate([hit, jnp.zeros((128 - count, 128), F32)], axis=0)
    choose = jnp.transpose(hit)[0 : 4 * peers, 0:count].astype(BF16)
    layers = [mxu(choose, recs[:, 16 + k, :].astype(BF16)) for k in range(6)]
    marks = mxu(choose, last.astype(BF16))
    marks = jnp.where(lanes((4 * peers, 128)) < 16, marks, 0.0)
    marks = [pltpu.roll(marks, 96, 1), pltpu.roll(marks, 112, 1)]
    row8, lane8 = rows((8, 128)), lanes((8, 128))
    upper, spare = row8 < 4, (row8 == 7) & (lane8 >= 96)
    for i in range(peers):
        tall = []
        for h, part in enumerate((high, low)):
            at = 4 * i + 2 * h
            seats = marks[0][at : at + 1] + marks[1][at + 1 : at + 2]
            tall.append(jnp.where(spare, seats, part))
        at = (i // 2) * 8
        for m in range(3):
            even, odd = layers[2 * m][at : at + 8], layers[2 * m + 1][at : at + 8]
            if i % 2 == 0:
                tall.append(jnp.where(upper, even, pltpu.roll(odd, 4, 0)))
            else:
                tall.append(jnp.where(upper, pltpu.roll(even, 4, 0), odd))
        out_ref[i] = jnp.concatenate(tall, axis=0).astype(BF16)


def spread(got_ref, out_ref):
    parts = jnp.sum(got_ref[:, 0:16, :].astype(F32), axis=0)
    share = parts[0:8] + parts[8:16]
    out_ref[...] = jnp.broadcast_to(share[None], out_ref.shape)


def place_records(got_ref, fp_ref, tp_ref, recs):
    recs[...] = got_ref[...].astype(F32)
    count = got_ref.shape[0]
    marks = [
        pltpu.roll(recs[:, 7 + 8 * (j // 2), :], 32 - 16 * (j % 2), 1) for j in range(4)
    ]
    marks = jnp.concatenate(marks, axis=0)
    lane = lanes((4 * count, 128))
    slot = jnp.sum(jnp.where(lane == 8, marks, 0.0), axis=1, keepdims=True) - 1.0
    hit = jnp.where((slot == lane.astype(F32)) & (lane < 8), 1.0, 0.0)
    hit = jnp.concatenate([hit, jnp.zeros((128 - 4 * count, 128), F32)], axis=0)
    choose = jnp.transpose(hit)[0:8, 0 : 4 * count].astype(BF16)
    for k in range(6):
        held = jnp.concatenate([recs[:, 16 + 4 * k + j, :] for j in range(4)], axis=0)
        got = mxu(choose, held.astype(BF16)).astype(BF16)
        f, y = (2 * k) // 4, (2 * k) % 4
        fp_ref[:, f, y, :] = got[:, 0:64]
        fp_ref[:, f, y + 1, :] = got[:, 64:128]
    tp_ref[...] = mxu(choose, marks.astype(BF16))[:, 0:6].astype(BF16)


def finish(
    got_ref, routed_ref,
    fp_ref, tp_ref, g1_ref, b1_ref, g2_ref, b2_ref, gs_ref, gf_ref, bf_ref, gt_ref, bt_ref,
    total, extra, second, recs,
):
    place_records(routed_ref, fp_ref, tp_ref, recs)
    swap = lax.axis_index("yh") * 8
    for p in range(16):
        block = got_ref[lax.rem(p + swap, 16)]
        total[p * 8 : p * 8 + 8] = block
        extra[p * 7 : p * 7 + 7] = block[0:7, 96:128]
    for kz in range(3):
        for ky in range(3):
            for kx in range(3):
                g = kz * 3 + kx
                at, to = 48 + 3 * (g // 2) + ky, 16 * (g % 2)
                g1_ref[(kz * 3 + ky) * 3 + kx] = extra[at : at + 1, to : to + 16]
    for ky in range(3):
        second[0:128] = total[0:128, ky * 32 : ky * 32 + 32]
        second[128:144] = extra[ky * 16 : ky * 16 + 16]
        for s, kx in enumerate((1, 2, 0)):
            for zo, kz in enumerate((1, 2, 0)):
                to = ((kz * 3 + ky) * 3 + kx) * 16
                part = second[s * 48 + zo * 16 : s * 48 + zo * 16 + 16]
                g2_ref[to : to + 16] = part
                if ky == 1 and kx == 1 and kz == 1:
                    gs_ref[...] = part
    gf_ref[...] = extra[63:66]
    b2_ref[...] = extra[66:67]
    b1_ref[...] = extra[67:68, 0:16]
    bf_ref[...] = extra[67:68, 16:19]
    bt_ref[...] = extra[67:68, 20:26]
    gt_ref[...] = extra[68:74]


SMEM = pl.BlockSpec(memory_space=pltpu.SMEM)
VMEM = pl.BlockSpec(memory_space=pltpu.VMEM)
MIB = 1024 * 1024


def run(kernel, name, scalars, arrays, outs, scratch=(), held=None, limit=16):
    return pl.pallas_call(
        kernel,
        out_shape=tuple(jax.ShapeDtypeStruct(*o[0:2]) for o in outs),
        in_specs=[SMEM] * len(scalars) + [held or VMEM] * len(arrays),
        out_specs=tuple(o[2] if len(o) > 2 else VMEM for o in outs),
        scratch_shapes=[pltpu.VMEM(*s) if isinstance(s, tuple) else s for s in scratch],
        compiler_params=pltpu.CompilerParams(vmem_limit_bytes=limit * MIB),
        name=name,
    )(*scalars, *arrays)


def exchange(block, axis, groups=None):
    return lax.all_to_all(block, axis, 0, 0, tiled=True, axis_index_groups=groups)


def on_device(
    volume, flux_target, tensor_target, dest,
    first_weight, first_bias, second_weight, second_bias, short_weight,
    flux_weight, flux_bias, tensor_weight, tensor_bias,
):
    depth, slabs = lax.axis_size("z"), lax.axis_size("slab")
    near, far = 2 * slabs, 2 * depth
    lines = [[z * 4 + y for z in range(depth) for y in pair] for pair in ((0, 3), (1, 2))]
    records = 8 * depth * 4
    flux_count = records * 3 * slabs * 4 * 64
    tensor_count = records * 6
    cell_count = slabs * 4 * 64
    place = lax.axis_index("slab").astype(jnp.int32).reshape(1)
    goal = jnp.pad(flux_target[:, :, 0], ((0, 0), (0, 1), (0, 0), (0, 64)))
    mine = jnp.concatenate([volume, goal.reshape(8, 2, 8, 128)], axis=1)
    record = exchange(mine, "slab")
    weights = run(
        prepare, "prepare", [place, dest, flux_bias],
        [
            jnp.transpose(first_weight[:, 0], (1, 2, 3, 0)),
            jnp.transpose(second_weight, (2, 3, 4, 1, 0)).reshape(432, 32),
            jnp.transpose(short_weight),
            flux_weight, tensor_weight,
            first_bias.reshape(1, 16), second_bias.reshape(1, 32), tensor_bias.reshape(1, 6),
            tensor_target,
        ],
        [
            ((512, 128), BF16), ((32, 512), BF16), ((128, 256), BF16), ((16, 128), BF16),
            ((32, 128), BF16), ((128, 128), BF16), ((128, 128), F32), ((40, 128), F32),
            ((256, CELLS), BF16),
        ],
        [((96, 128), F32), ((512, 128), F32)],
    )
    (terms,) = run(
        functools.partial(step, 2.0 / flux_count, 2.0 / tensor_count, float(cell_count)),
        "step", [], [record, *weights], [((near, SENT, 128), BF16)],
        [
            ((9 * BLOCK, CELLS), BF16), ((128, CELLS), BF16), ((640, CELLS), BF16),
            ((CELLS, CELLS), BF16), ((ROWS, 128), F32), ((112, 128), F32),
            ((near, SENT, 128), F32),
        ],
    )
    terms = exchange(terms, ("yl", "slab"))
    (routed,) = run(
        route, "route", [], [terms], [((far, ROUTED, 128), BF16)],
        [((near, SENT, 128), F32)],
    )
    routed = exchange(routed, ("z", "yh", "yl"), lines)
    (share,) = run(spread, "spread", [], [routed], [((near, 8, 128), F32)])
    total = exchange(share, ("yl", "slab"))
    fp, tp, g1, b1, g2, b2, gs, gf, bf, gt, bt = run(
        finish, "finish", [], [total, routed],
        [
            ((8, 3, 4, 64), BF16), ((8, 6), BF16),
            ((27, 1, 16), F32), ((1, 16), F32), ((432, 32), F32), ((1, 32), F32),
            ((16, 32), F32), ((3, 32), F32), ((1, 3), F32), ((6, 32), F32), ((1, 6), F32),
        ],
        [
            ((ROWS, 128), F32), ((112, 32), F32), ((BLOCK, 32), F32),
            ((far, ROUTED, 128), F32),
        ],
    )
    return (
        fp[:, :, None],
        tp,
        jnp.transpose(g1.reshape(3, 3, 3, 1, 16), (4, 3, 0, 1, 2)),
        b1.reshape(16),
        jnp.transpose(g2.reshape(3, 3, 3, 16, 32), (4, 3, 0, 1, 2)),
        b2.reshape(32),
        jnp.transpose(gs),
        gf,
        bf.reshape(3),
        gt,
        bt.reshape(6),
    )


def solution(mesh):
    grid = mesh.devices.reshape(-1, 2, 2, mesh.shape["slab"])
    mesh = jax.sharding.Mesh(grid, ("z", "yh", "yl", "slab"))
    groups = ("z", "yh", "yl")
    cells = P(groups, "slab", None, None)
    fields = P(groups, None, "slab", None, None)
    return jax.shard_map(
        on_device,
        mesh=mesh,
        in_specs=(cells, fields, P(groups, None), P(groups)) + (P(),) * 9,
        out_specs=(fields, P(groups, None)) + (P(),) * 9,
        check_vma=False,
    )
```

```python
import functools

import jax
import jax.numpy as jnp
from jax import lax
from jax.experimental import pallas as pl
from jax.experimental.pallas import tpu as pltpu
from jax.sharding import PartitionSpec as P

F32 = jnp.float32
BF16 = jnp.bfloat16
NN = (((1,), (0,)), ((), ()))
NT = (((1,), (1,)), ((), ()))
TN = (((0,), (0,)), ((), ()))

BLOCK = 144
CELLS = 512
TAPS = 144
ROWS = 128
SENT = 24
ROUTED = 32


def mxu(a, b, dims=NN):
    return lax.dot_general(a, b, dims, preferred_element_type=F32)


def lanes(shape):
    return lax.broadcasted_iota(jnp.int32, shape, len(shape) - 1)


def rows(shape):
    return lax.broadcasted_iota(jnp.int32, shape, len(shape) - 2)


def side_of(y):
    return ((y + 1) // 2) % 2


def prepare(
    place_ref, dest_ref, bf_ref,
    w1_ref, w2_ref, ws_ref, wf_ref, wt_ref, b1_ref, b2_ref, bt_ref, kt_ref,
    t1_ref, w2a_ref, wb_ref, wsb_ref, fw_ref, fwt_ref, cols_ref, wtt_ref, pick_ref,
    base, order,
):
    r, c = rows((256, CELLS)), lanes((256, CELLS))
    x = 2 * (c % 64) - 1 + c // 128
    pick = (r % 128 == x) & (r // 128 == (c % 128) // 64)
    pick_ref[...] = jnp.where(pick, 1.0, 0.0).astype(BF16)
    base[...] = jnp.zeros_like(base)
    for kz in range(3):
        for ky in range(3):
            for kx in range(3):
                at = kz * 32 + kx * 8 + ky
                base[at : at + 1, 0:16] = w1_ref[kz, ky, kx : kx + 1, :].astype(F32)
    taps = base[0:88]
    placed = jnp.zeros((128, 128), F32)
    for px in range(2):
        for z in range(2):
            down, right = z * 32 + px * 8, px * 32 + z * 16
            parts = [pltpu.roll(taps, right, 1) if right else taps]
            if down < 40:
                parts = parts + [jnp.zeros((40 - down, 128), F32)]
            if down:
                parts = [jnp.zeros((down, 128), F32)] + parts
            placed = placed + jnp.concatenate(parts, axis=0)
    across = jnp.transpose(placed)[0:64]
    place = lanes((64, 128)) % 8
    for y in range(8):
        own = across
        if y == 0:
            own = jnp.where(place == 0, 0.0, own)
        if y == 7:
            own = jnp.where(place == 2, 0.0, own)
        if y != 1:
            own = pltpu.roll(own, (y - 1) % 128, 1)
        t1_ref[y * 64 : y * 64 + 64, :] = own.astype(BF16)
    order[...] = jnp.zeros_like(order)
    w2 = w2_ref[...].astype(F32)
    for ky in range(3):
        for s, kx in enumerate((1, 2, 0)):
            for zo, kz in enumerate((1, 2, 0)):
                to, at = ky * 144 + s * 48 + zo * 16, ((kz * 3 + ky) * 3 + kx) * 16
                order[to : to + 16, 0:32] = w2[at : at + 16]
    order[432:448, 0:32] = ws_ref[...].astype(F32)
    w2t = order[...]
    w2a_ref[...] = jnp.transpose(w2t)[0:32].astype(BF16)
    wsb_ref[...] = w2t[432:448].astype(BF16)
    own, near = ((1, 0),), ((2, 0), (0, 1))
    for sub in range(2):
        for px in range(2):
            for z in range(2):
                sides = [jnp.zeros((16, 128), F32), jnp.zeros((16, 128), F32)]
                for ky, sy in near if sub else own:
                    for kx, sx in near if px else own:
                        for kz, sz in near if z else own:
                            at = ky * 144 + (1, 2, 0).index(kx) * 48 + (1, 2, 0).index(kz) * 16
                            to = sz * 64 + sx * 32
                            part = w2t[at : at + 16]
                            sides[sy] = sides[sy] + (pltpu.roll(part, to, 1) if to else part)
                to = sub * 64 + px * 32 + z * 16
                wb_ref[to : to + 16, :] = jnp.concatenate(sides, axis=1).astype(BF16)
    base[...] = jnp.zeros_like(base)
    base[0:3, 0:32] = wf_ref[...].astype(F32)
    wide = base[0:8, :]
    wide = wide + pltpu.roll(wide, 32, 1)
    wide = wide + pltpu.roll(wide, 64, 1)
    head = jnp.concatenate(
        [jnp.broadcast_to(wide[f : f + 1], (8, 128)) for f in range(3)]
        + [jnp.zeros((104, 128), F32)],
        axis=0,
    )
    mine = (lanes((128, 128)) // 32 == rows((128, 128)) % 8) & (rows((128, 128)) < 24)
    head = jnp.where(mine, head, 0.0)
    fw_ref[...] = head[0:32].astype(BF16)
    fwt_ref[...] = jnp.transpose(head).astype(BF16)
    base[...] = jnp.zeros_like(base)
    base[0:1, 0:16] = b1_ref[...]
    base[1:2, 0:32] = b2_ref[...]
    base[8:14, 0:32] = wt_ref[...].astype(F32)
    pad = jnp.zeros((120, 128), F32)
    cols_ref[...] = jnp.transpose(jnp.concatenate([base[0:8, :], pad], axis=0))
    wtt_ref[0:32] = jnp.transpose(jnp.concatenate([base[8:16, :], pad], axis=0))[0:32]
    base[16:24, 0:6] = kt_ref[...].astype(F32)
    wtt_ref[32:40] = jnp.zeros((8, 128), F32)
    wtt_ref[32:33, 0:6] = bt_ref[...]
    place = place_ref[0]
    mine = rows((8, 128)) == place
    wtt_ref[33:34] = jnp.sum(jnp.where(mine, base[16:24], 0.0), axis=0, keepdims=True)
    dest = dest_ref[place]
    group = jnp.maximum(dest, 0) // 8
    live = jnp.where(dest >= 0, 1.0, 0.0)
    wtt_ref[34:35] = jnp.broadcast_to(live, (1, 128))
    wtt_ref[35:36] = jnp.broadcast_to(dest.astype(F32), (1, 128))
    for t in range(2):
        leads = side_of(lax.axis_index("yh") * 2 + t) == side_of(group % 4)
        here = jnp.where((dest >= 0) & leads, 1.0, 0.0)
        wtt_ref[36 + t : 37 + t] = jnp.broadcast_to(here, (1, 128))
    rank = jnp.float32(0)
    for e in range(8):
        other = dest_ref[e]
        twin = (other >= 0) & (jnp.maximum(other, 0) // 8 == group) & (e < place)
        rank = jnp.where(twin, 1.0, rank)
    wtt_ref[38:39] = jnp.broadcast_to(rank, (1, 128))
    row = rows((128, 1))
    bias = jnp.where(row < 8, bf_ref[0], jnp.where(row < 16, bf_ref[1], bf_ref[2]))
    cols_ref[:, 2:3] = bias


def step(
    flux_scale, tensor_scale, cell_count,
    got_ref,
    t1_ref, w2a_ref, wb_ref, wsb_ref, fw_ref, fwt_ref, cols_ref, wtt_ref, pick_ref,
    out_ref,
    a_ref, a2_ref, d_ref, dz1_ref, total, extra, sent,
):
    live = wtt_ref[34:35, 0:1]
    empty = jnp.zeros((8, 128), F32)

    def plane(z):
        if z < 0 or z > 15:
            return empty
        return got_ref[z // 2, z % 2].astype(F32)

    low = jnp.concatenate([plane(4 * q - 1 + zi) for zi in range(4) for q in range(4)], axis=0)
    high = jnp.concatenate([plane(4 * q + 1 + zi) for zi in range(4) for q in range(4)], axis=0)
    cells = jnp.concatenate([low, high], axis=1).astype(BF16)
    apart = mxu(cells, pick_ref[...])
    lines = []
    for zi in range(4):
        for xt in range(4):
            lines.append(
                jnp.concatenate(
                    [
                        apart[zi * 32 + q * 8 : zi * 32 + q * 8 + 8, xt * 128 : xt * 128 + 128]
                        for q in range(4)
                    ],
                    axis=1,
                )
            )
    lines.append(jnp.where(rows((16, CELLS)) == 0, 1.0, 0.0))
    xcol = jnp.concatenate(lines, axis=0).astype(BF16)
    b1 = jnp.concatenate([cols_ref[0:16, 0:1]] * 4, axis=0)
    zero = jnp.zeros((), BF16)
    first_z = lanes((16, CELLS)) < 64
    first_x = lanes((48, CELLS)) % 64 == 0
    a_ref[0:BLOCK] = jnp.zeros((BLOCK, CELLS), BF16)
    z1_all = mxu(t1_ref[...], xcol[0:128])
    for y in range(8):
        z1 = z1_all[y * 64 : y * 64 + 64] + b1
        act = jnp.maximum(z1, 0.0).astype(BF16)
        at = (y + 1) * BLOCK
        for px in range(2):
            moved = pltpu.roll(act[px * 32 + 16 : px * 32 + 32], 64, 1)
            moved = jnp.where(first_z, zero, moved)
            a_ref[at + px * 48 : at + px * 48 + 32] = act[px * 32 : px * 32 + 32]
            a_ref[at + px * 48 + 32 : at + px * 48 + 48] = moved
        late = jnp.concatenate([act[32:64], moved], axis=0)
        a_ref[at + 96 : at + BLOCK] = jnp.where(first_x, zero, pltpu.roll(late, 1, 1))
    b2 = cols_ref[0:32, 1:2]
    pooled = jnp.zeros((32, 1), F32)
    for y in range(4):
        at = 2 * y * BLOCK
        z2 = mxu(w2a_ref[:, 0:432], a_ref[at : at + 432])
        short = mxu(w2a_ref[:, 432:448], a_ref[at + BLOCK : at + BLOCK + 16])
        z2 = (z2 + b2) + short
        act = jnp.maximum(z2, 0.0).astype(BF16)
        a2_ref[y * 32 : y * 32 + 32] = act
        pooled = pooled + jnp.sum(act.astype(F32), axis=1, keepdims=True)
    pooled = pooled / cell_count
    a2 = a2_ref[...]
    head = wtt_ref[0:32]
    tensor = jnp.sum(head * pooled, axis=0, keepdims=True) + wtt_ref[32:33]
    dt = tensor_scale * (tensor - wtt_ref[33:34]) * live
    spread = jnp.sum(head * dt, axis=1, keepdims=True) / cell_count
    row = rows((24, 1))
    full = mxu(fw_ref[0:24], a2) + cols_ref[0:24, 2:3]
    goals = [
        jnp.concatenate(
            [
                got_ref[2 * q, 2 + h].astype(F32)
                + pltpu.roll(got_ref[2 * q + 1, 2 + h].astype(F32), 64, 1)
                for q in range(4)
            ],
            axis=1,
        )
        for h in range(2)
    ]
    wanted = jnp.concatenate([goals[0], pltpu.roll(goals[0], 4, 0), goals[1]], axis=0)
    diff = flux_scale * (full - wanted) * live
    df = jnp.where(row % 8 < 4, diff, 0.0)
    df = jnp.concatenate([df, jnp.zeros((8, CELLS), F32)], axis=0).astype(BF16)
    member = lanes((8, CELLS)) // 64 == rows((8, CELLS))
    shares = []
    for f in range(3):
        for y in range(4):
            line = jnp.where(member, full[f * 8 + y : f * 8 + y + 1], 0.0)
            line = (line[:, 0:128] + line[:, 128:256]) + (line[:, 256:384] + line[:, 384:512])
            shares.append(line + pltpu.roll(line, 64, 1))
    left = lanes((8, 128)) < 64
    lane8 = lanes((8, 128))
    dest = wtt_ref[35:36]
    slot = dest - 8.0 * jnp.floor(dest / 8.0) + 1.0
    last = jnp.where(lane8 < 6, jnp.broadcast_to(tensor, (8, 128)), 0.0)
    last = jnp.where(lane8 == 6, dest, last)
    last = jnp.where(lane8 == 7, wtt_ref[38:39], last)
    last = jnp.where(lane8 == 8, slot, last)
    for t in range(2):
        here = wtt_ref[36 + t : 37 + t] > 0
        for k in range(6):
            both = jnp.where(left, shares[2 * k], shares[2 * k + 1])
            sent[t * 8 : t * 8 + 8, 16 + k, :] = jnp.where(here, both, 0.0)
        sent[t * 8 : t * 8 + 8, 22, :] = jnp.where(
            here, last, jnp.where(lane8 == 6, -1.0, 0.0)
        )
        sent[t * 8 : t * 8 + 8, 23, :] = jnp.zeros((8, 128), F32)
    last_x = lanes((32, CELLS)) % 64 == 63
    last_z = lanes((32, CELLS)) >= 448
    bias2 = jnp.zeros((32, 1), F32)
    dz2 = []
    for y in range(4):
        da2 = mxu(fwt_ref[y * 32 : y * 32 + 32, 0:32], df) + spread
        d = jnp.where(a2_ref[y * 32 : y * 32 + 32] > 0, da2, 0.0).astype(BF16)
        wide = d.astype(F32)
        bias2 = bias2 + jnp.sum(wide, axis=1, keepdims=True)
        next_x = jnp.where(last_x, zero, pltpu.roll(d, CELLS - 1, 1))
        next_z = jnp.where(last_z, zero, pltpu.roll(d, CELLS - 64, 1))
        both = jnp.where(last_x | last_z, zero, pltpu.roll(d, CELLS - 65, 1))
        d_ref[y * 128 : y * 128 + 32] = d
        d_ref[y * 128 + 32 : y * 128 + 64] = next_x
        d_ref[y * 128 + 64 : y * 128 + 96] = next_z
        d_ref[y * 128 + 96 : y * 128 + 128] = both
        dz2.append(d)
    d_ref[512:640] = jnp.zeros((128, CELLS), BF16)
    none = jnp.zeros((32, CELLS), BF16)
    second = jnp.zeros((BLOCK, 128), F32)
    for y in range(4):
        at = (2 * y + 1) * BLOCK
        da1 = mxu(wb_ref[...], d_ref[y * 128 : y * 128 + 256])
        short = mxu(wsb_ref[:, 0:32], dz2[y])
        da1 = jnp.concatenate([da1[0:16] + short, da1[16:128]], axis=0)
        for sub in range(2):
            act = a_ref[at + sub * BLOCK : at + sub * BLOCK + BLOCK]
            if sub == 0:
                sides = [none, dz2[y], none, none]
            else:
                sides = [dz2[y + 1] if y < 3 else none, none, dz2[y], none]
            second = second + mxu(act, jnp.concatenate(sides, axis=0), NT)
            on = jnp.concatenate([act[0:32], act[48:80]], axis=0) > 0
            dz1 = jnp.where(on, da1[sub * 64 : sub * 64 + 64], 0.0).astype(BF16)
            dz1_ref[(2 * y + sub) * 64 : (2 * y + sub) * 64 + 64] = dz1
    parts = mxu(dz1_ref[...], xcol, NT)
    place8 = lanes((64, 128)) % 8
    fold = jnp.zeros((64, 128), F32)
    tail = jnp.zeros((64, 1), F32)
    for y in range(8):
        part = parts[y * 64 : y * 64 + 64, 0:128]
        tail = tail + parts[y * 64 : y * 64 + 64, 128:129]
        if y == 0:
            part = jnp.where(place8 == 7, 0.0, part)
        if y == 7:
            part = jnp.where(place8 == 0, 0.0, part)
        if y != 1:
            part = pltpu.roll(part, (1 - y) % 128, 1)
        fold = fold + part
    first = jnp.zeros((16, 128), F32)
    first_bias = jnp.zeros((16, 1), F32)
    for px in range(2):
        for z in range(2):
            at, left = px * 32 + z * 16, z * 32 + px * 8
            part = fold[at : at + 16]
            first = first + (pltpu.roll(part, 128 - left, 1) if left else part)
            first_bias = first_bias + tail[at : at + 16]
    lane = lanes((1, 128))
    bias2 = jnp.where(lanes((32, 128)) == 0, bias2, pooled * pltpu.roll(dt, 1, 1))
    upright = jnp.concatenate(
        [
            jnp.where(lanes((16, 128)) == 127, first_bias, first),
            jnp.zeros((16, 128), F32),
            bias2,
            jnp.zeros((64, 128), F32),
        ],
        axis=0,
    )
    upright = jnp.transpose(upright)
    cross = mxu(df, a2, NT)
    same = lanes((32, 128)) // 32 == rows((32, 128)) % 8
    cross = jnp.where(same, cross, 0.0)
    cross = cross + pltpu.roll(cross, 64, 1)
    cross = cross + pltpu.roll(cross, 32, 1)
    flux_sum = jnp.sum(df.astype(F32), axis=1, keepdims=True)
    for ky in range(3):
        tail_block = pltpu.roll(second[128:144], (96 - ky * 32) % 128, 1)
        extra[ky * 16 : ky * 16 + 16] = tail_block
    lane8 = lanes((8, 128))
    for i in range(5):
        pair = jnp.zeros((8, 128), F32)
        for h in range(2 if i < 4 else 1):
            g = 2 * i + h
            at = (g // 3) * 32 + (g % 3) * 8
            part = jnp.where(lane8 < 16, upright[at : at + 8], 0.0)
            pair = pair + pltpu.roll(part, 96 + 16 * h, 1)
        extra[48 + 3 * i : 51 + 3 * i] = pair[0:3]
    bias_row = jnp.zeros((1, 128), F32)
    for f in range(3):
        extra[63 + f : 64 + f] = jnp.sum(cross[f * 8 : f * 8 + 8], axis=0, keepdims=True)
        sums = jnp.sum(flux_sum[f * 8 : f * 8 + 8], axis=0, keepdims=True)
        bias_row = jnp.where(lane == 112 + f, sums, bias_row)
    extra[66:67] = pltpu.roll(upright[0:1], 64, 1)
    first_row = pltpu.roll(jnp.where(lane < 16, upright[127:128], 0.0), 96, 1)
    tensor_row = pltpu.roll(jnp.where(lane < 6, dt, 0.0), 116, 1)
    extra[67:68] = first_row + bias_row + tensor_row
    extra[68:74] = pltpu.roll(upright[0:8], 64, 1)[1:7]
    extra[74:80] = jnp.zeros((6, 128), F32)
    rest = lane8 >= 96
    swap = lax.axis_index("yh") * 8
    for t in range(16):
        block = second[t * 8 : t * 8 + 8]
        total[t * 8 : t * 8 + 8] = jnp.where(rest, 0.0, block)
        tail_rows = extra[t * 3 : t * 3 + 3]
        other_rows = extra[48 + t * 2 : 50 + t * 2]
        total[t * 8 : t * 8 + 3] = jnp.where(rest[0:3], tail_rows, block[0:3])
        total[t * 8 + 3 : t * 8 + 5] = jnp.where(rest[0:2], other_rows, block[3:5])
        block = total[t * 8 : t * 8 + 8]
        high = block.astype(BF16).astype(F32)
        to = lax.rem(t + swap, 16)
        sent[to, 0:8, :] = high
        sent[to, 8:16, :] = block - high
    out_ref[...] = sent[...].astype(BF16)


def route(got_ref, out_ref, recs):
    recs[...] = got_ref[...].astype(F32)
    count = got_ref.shape[0]
    full = recs[0, 0:8, :] + recs[0, 8:16, :]
    for p in range(1, count):
        full = full + (recs[p, 0:8, :] + recs[p, 8:16, :])
    high = full.astype(BF16).astype(F32)
    low = full - high
    peers = out_ref.shape[0]
    lane = lanes((count, 128))
    last = recs[:, 22, :]
    dest = jnp.sum(jnp.where(lane == 6, last, 0.0), axis=1, keepdims=True).astype(jnp.int32)
    rank = jnp.sum(jnp.where(lane == 7, last, 0.0), axis=1, keepdims=True).astype(jnp.int32)
    side = side_of(lax.axis_index("yh") * 2 + lax.axis_index("yl"))
    peer = lane // 4
    group = (peer // 2) * 4 + jnp.where(peer % 2 == 0, side, 3 - side)
    seat = (rows((count, 128)) // 8) * 2 + rank
    right = (dest >= group * 8) & (dest < group * 8 + 8) & (seat == lane % 4)
    hit = jnp.where(right & (peer < peers), 1.0, 0.0)
    hit = jnp.concatenate([hit, jnp.zeros((128 - count, 128), F32)], axis=0)
    choose = jnp.transpose(hit)[0 : 4 * peers, 0:count].astype(BF16)
    layers = [mxu(choose, recs[:, 16 + k, :].astype(BF16)) for k in range(6)]
    marks = mxu(choose, last.astype(BF16))
    lane = lanes((4 * peers, 128))
    marks = jnp.where(lane == 6, pltpu.roll(marks, 126, 1), jnp.where(lane < 6, marks, 0.0))
    marks = [pltpu.roll(marks, 96 + 8 * j, 1) for j in range(4)]
    row8, lane8 = rows((8, 128)), lanes((8, 128))
    upper, spare = row8 < 4, (row8 == 7) & (lane8 >= 96)
    remainder = ((row8 == 5) | (row8 == 6)) & (lane8 >= 96)
    share = jnp.where(remainder, pltpu.roll(low, 2, 0), high)
    for i in range(peers):
        seats = marks[0][4 * i : 4 * i + 1]
        for j in range(1, 4):
            seats = seats + marks[j][4 * i + j : 4 * i + j + 1]
        tall = [jnp.where(spare, seats, share)]
        at = (i // 2) * 8
        for m in range(3):
            even, odd = layers[2 * m][at : at + 8], layers[2 * m + 1][at : at + 8]
            if i % 2 == 0:
                tall.append(jnp.where(upper, even, pltpu.roll(odd, 4, 0)))
            else:
                tall.append(jnp.where(upper, pltpu.roll(even, 4, 0), odd))
        out_ref[i] = jnp.concatenate(tall, axis=0).astype(BF16)


def spread(got_ref, out_ref):
    parts = jnp.sum(got_ref[:, 0:8, :].astype(F32), axis=0)
    row8 = rows((8, 128))
    split = ((row8 == 3) | (row8 == 4)) & (lanes((8, 128)) >= 96)
    share = parts + jnp.where(split, pltpu.roll(parts, 6, 0), 0.0)
    out_ref[...] = jnp.broadcast_to(share[None], out_ref.shape)


def pick_records(got_ref, recs):
    recs[...] = got_ref[...].astype(F32)
    count = got_ref.shape[0]
    marks = [pltpu.roll(recs[:, 7, :], 32 - 8 * j, 1) for j in range(4)]
    marks = jnp.concatenate(marks, axis=0)
    lane = lanes((4 * count, 128))
    slot = jnp.sum(jnp.where(lane == 6, marks, 0.0), axis=1, keepdims=True) - 1.0
    hit = jnp.where((slot == lane.astype(F32)) & (lane < 8), 1.0, 0.0)
    hit = hit.astype(BF16)
    held = [
        jnp.concatenate([recs[:, 8 + 4 * k + j, :] for j in range(4)], axis=0)
        for k in range(6)
    ]
    every = mxu(hit, jnp.concatenate(held + [marks], axis=1).astype(BF16), TN)[0:8]
    return every


def finish(
    got_ref, routed_ref,
    fp_ref, tp_ref, g1_ref, b1_ref, g2_ref, b2_ref, gs_ref, gf_ref, bf_ref, gt_ref, bt_ref,
    total, extra, second, recs,
):
    every = pick_records(routed_ref, recs)
    swap = lax.axis_index("yh") * 8
    for p in range(16):
        block = got_ref[lax.rem(p + swap, 16)]
        total[p * 8 : p * 8 + 8] = block
        extra[p * 3 : p * 3 + 3] = block[0:3, 96:128]
        extra[48 + p * 2 : 50 + p * 2] = block[3:5, 96:128]
    for kz in range(3):
        for ky in range(3):
            for kx in range(3):
                g = kz * 3 + kx
                at, to = 48 + 3 * (g // 2) + ky, 16 * (g % 2)
                g1_ref[(kz * 3 + ky) * 3 + kx] = extra[at : at + 1, to : to + 16]
    for ky in range(3):
        second[0:128] = total[0:128, ky * 32 : ky * 32 + 32]
        second[128:144] = extra[ky * 16 : ky * 16 + 16]
        for s, kx in enumerate((1, 2, 0)):
            for zo, kz in enumerate((1, 2, 0)):
                to = ((kz * 3 + ky) * 3 + kx) * 16
                part = second[s * 48 + zo * 16 : s * 48 + zo * 16 + 16]
                g2_ref[to : to + 16] = part
                if ky == 1 and kx == 1 and kz == 1:
                    gs_ref[...] = part
    gf_ref[...] = extra[63:66]
    b2_ref[...] = extra[66:67]
    b1_ref[...] = extra[67:68, 0:16]
    bf_ref[...] = extra[67:68, 16:19]
    bt_ref[...] = extra[67:68, 20:26]
    gt_ref[...] = extra[68:74]
    for k in range(6):
        got = every[:, k * 128 : k * 128 + 128].astype(BF16)
        f, y = (2 * k) // 4, (2 * k) % 4
        fp_ref[:, f, y, :] = got[:, 0:64]
        fp_ref[:, f, y + 1, :] = got[:, 64:128]
    tp_ref[...] = every[:, 768:774].astype(BF16)


SMEM = pl.BlockSpec(memory_space=pltpu.SMEM)
VMEM = pl.BlockSpec(memory_space=pltpu.VMEM)
MIB = 1024 * 1024


def run(kernel, name, scalars, arrays, outs, scratch=(), held=None, limit=16):
    return pl.pallas_call(
        kernel,
        out_shape=tuple(jax.ShapeDtypeStruct(*o[0:2]) for o in outs),
        in_specs=[SMEM] * len(scalars) + [held or VMEM] * len(arrays),
        out_specs=tuple(o[2] if len(o) > 2 else VMEM for o in outs),
        scratch_shapes=[pltpu.VMEM(*s) if isinstance(s, tuple) else s for s in scratch],
        compiler_params=pltpu.CompilerParams(vmem_limit_bytes=limit * MIB),
        name=name,
    )(*scalars, *arrays)


def exchange(block, axis, groups=None):
    return lax.all_to_all(block, axis, 0, 0, tiled=True, axis_index_groups=groups)


def on_device(
    volume, flux_target, tensor_target, dest,
    first_weight, first_bias, second_weight, second_bias, short_weight,
    flux_weight, flux_bias, tensor_weight, tensor_bias,
):
    depth, slabs = lax.axis_size("z"), lax.axis_size("slab")
    near, far = 2 * slabs, 2 * depth
    lines = [[z * 4 + y for z in range(depth) for y in pair] for pair in ((0, 3), (1, 2))]
    records = 8 * depth * 4
    flux_count = records * 3 * slabs * 4 * 64
    tensor_count = records * 6
    cell_count = slabs * 4 * 64
    place = lax.axis_index("slab").astype(jnp.int32).reshape(1)
    goal = jnp.pad(flux_target[:, :, 0], ((0, 0), (0, 1), (0, 0), (0, 64)))
    mine = jnp.concatenate([volume, goal.reshape(8, 2, 8, 128)], axis=1)
    record = exchange(mine, "slab")
    weights = run(
        prepare, "prepare", [place, dest, flux_bias],
        [
            jnp.transpose(first_weight[:, 0], (1, 2, 3, 0)),
            jnp.transpose(second_weight, (2, 3, 4, 1, 0)).reshape(432, 32),
            jnp.transpose(short_weight),
            flux_weight, tensor_weight,
            first_bias.reshape(1, 16), second_bias.reshape(1, 32), tensor_bias.reshape(1, 6),
            tensor_target,
        ],
        [
            ((512, 128), BF16), ((32, 512), BF16), ((128, 256), BF16), ((16, 128), BF16),
            ((32, 128), BF16), ((128, 128), BF16), ((128, 128), F32), ((40, 128), F32),
            ((256, CELLS), BF16),
        ],
        [((96, 128), F32), ((512, 128), F32)],
    )
    (terms,) = run(
        functools.partial(step, 2.0 / flux_count, 2.0 / tensor_count, float(cell_count)),
        "step", [], [record, *weights], [((near, SENT, 128), BF16)],
        [
            ((9 * BLOCK, CELLS), BF16), ((128, CELLS), BF16), ((640, CELLS), BF16),
            ((CELLS, CELLS), BF16), ((ROWS, 128), F32), ((112, 128), F32),
            ((near, SENT, 128), F32),
        ],
    )
    terms = exchange(terms, ("yl", "slab"))
    (routed,) = run(
        route, "route", [], [terms], [((far, ROUTED, 128), BF16)],
        [((near, SENT, 128), F32)],
    )
    routed = exchange(routed, ("z", "yh", "yl"), lines)
    (share,) = run(spread, "spread", [], [routed], [((near, 8, 128), F32)])
    total = exchange(share, ("yl", "slab"))
    fp, tp, g1, b1, g2, b2, gs, gf, bf, gt, bt = run(
        finish, "finish", [], [total, routed],
        [
            ((8, 3, 4, 64), BF16), ((8, 6), BF16),
            ((27, 1, 16), F32), ((1, 16), F32), ((432, 32), F32), ((1, 32), F32),
            ((16, 32), F32), ((3, 32), F32), ((1, 3), F32), ((6, 32), F32), ((1, 6), F32),
        ],
        [
            ((ROWS, 128), F32), ((112, 32), F32), ((BLOCK, 32), F32),
            ((far, ROUTED, 128), F32),
        ],
    )
    return (
        fp[:, :, None],
        tp,
        jnp.transpose(g1.reshape(3, 3, 3, 1, 16), (4, 3, 0, 1, 2)),
        b1.reshape(16),
        jnp.transpose(g2.reshape(3, 3, 3, 16, 32), (4, 3, 0, 1, 2)),
        b2.reshape(32),
        jnp.transpose(gs),
        gf,
        bf.reshape(3),
        gt,
        bt.reshape(6),
    )


def solution(mesh):
    grid = mesh.devices.reshape(-1, 2, 2, mesh.shape["slab"])
    mesh = jax.sharding.Mesh(grid, ("z", "yh", "yl", "slab"))
    groups = ("z", "yh", "yl")
    cells = P(groups, "slab", None, None)
    fields = P(groups, None, "slab", None, None)
    return jax.shard_map(
        on_device,
        mesh=mesh,
        in_specs=(cells, fields, P(groups, None), P(groups)) + (P(),) * 9,
        out_specs=(fields, P(groups, None)) + (P(),) * 9,
        check_vma=False,
    )
```

```python
import functools

import jax
import jax.numpy as jnp
from jax import lax
from jax.experimental import pallas as pl
from jax.experimental.pallas import tpu as pltpu
from jax.sharding import PartitionSpec as P

F32 = jnp.float32
BF16 = jnp.bfloat16
NN = (((1,), (0,)), ((), ()))
NT = (((1,), (1,)), ((), ()))
TN = (((0,), (0,)), ((), ()))

BLOCK = 144
TALL = 160
CELLS = 512
TAPS = 144
ROWS = 128
SENT = 16
ROUTED = 32


def mxu(a, b, dims=NN):
    return lax.dot_general(a, b, dims, preferred_element_type=F32)


def lanes(shape):
    return lax.broadcasted_iota(jnp.int32, shape, len(shape) - 1)


def rows(shape):
    return lax.broadcasted_iota(jnp.int32, shape, len(shape) - 2)


def side_of(y):
    return ((y + 1) // 2) % 2


def prepare(
    place_ref, dest_ref, bf_ref,
    w1_ref, w2_ref, ws_ref, wf_ref, wt_ref, b1_ref, b2_ref, bt_ref, kt_ref,
    t1_ref, w2a_ref, wb_ref, wsb_ref, fw_ref, fwt_ref, cols_ref, wtt_ref, pick_ref,
    base, order,
):
    r, c = rows((256, CELLS)), lanes((256, CELLS))
    x = 2 * (c % 64) - 1 + c // 128
    pick = (r % 128 == x) & (r // 128 == (c % 128) // 64)
    pick_ref[...] = jnp.where(pick, 1.0, 0.0).astype(BF16)
    base[...] = jnp.zeros_like(base)
    for kz in range(3):
        for ky in range(3):
            for kx in range(3):
                at = kz * 32 + kx * 8 + ky
                base[at : at + 1, 0:16] = w1_ref[kz, ky, kx : kx + 1, :].astype(F32)
    taps = base[0:88]
    placed = jnp.zeros((128, 128), F32)
    for px in range(2):
        for z in range(2):
            down, right = z * 32 + px * 8, px * 32 + z * 16
            parts = [pltpu.roll(taps, right, 1) if right else taps]
            if down < 40:
                parts = parts + [jnp.zeros((40 - down, 128), F32)]
            if down:
                parts = [jnp.zeros((down, 128), F32)] + parts
            placed = placed + jnp.concatenate(parts, axis=0)
    across = jnp.transpose(placed)[0:64]
    place = lanes((64, 128)) % 8
    for y in range(8):
        own = across
        if y == 0:
            own = jnp.where(place == 0, 0.0, own)
        if y == 7:
            own = jnp.where(place == 2, 0.0, own)
        if y != 1:
            own = pltpu.roll(own, (y - 1) % 128, 1)
        t1_ref[y * 64 : y * 64 + 64, :] = own.astype(BF16)
    order[...] = jnp.zeros_like(order)
    w2 = w2_ref[...].astype(F32)
    for ky in range(3):
        for s, kx in enumerate((1, 2, 0)):
            for zo, kz in enumerate((1, 2, 0)):
                to, at = ky * TALL + s * 48 + zo * 16, ((kz * 3 + ky) * 3 + kx) * 16
                order[to : to + 16, 0:32] = w2[at : at + 16]
    order[304:320, 0:32] = ws_ref[...].astype(F32)
    w2t = order[...]
    w2a_ref[...] = jnp.transpose(w2t)[0:32].astype(BF16)
    wsb_ref[...] = w2t[304:320].astype(BF16)
    own, near = ((1, 0),), ((2, 0), (0, 1))
    for sub in range(2):
        for px in range(2):
            for z in range(2):
                sides = [jnp.zeros((16, 128), F32), jnp.zeros((16, 128), F32)]
                for ky, sy in near if sub else own:
                    for kx, sx in near if px else own:
                        for kz, sz in near if z else own:
                            at = ky * TALL + (1, 2, 0).index(kx) * 48 + (1, 2, 0).index(kz) * 16
                            to = sz * 64 + sx * 32
                            part = w2t[at : at + 16]
                            sides[sy] = sides[sy] + (pltpu.roll(part, to, 1) if to else part)
                to = sub * 64 + px * 32 + z * 16
                wb_ref[to : to + 16, :] = jnp.concatenate(sides, axis=1).astype(BF16)
    base[...] = jnp.zeros_like(base)
    base[0:3, 0:32] = wf_ref[...].astype(F32)
    wide = base[0:8, :]
    wide = wide + pltpu.roll(wide, 32, 1)
    wide = wide + pltpu.roll(wide, 64, 1)
    head = jnp.concatenate(
        [jnp.broadcast_to(wide[f : f + 1], (8, 128)) for f in range(3)]
        + [jnp.zeros((104, 128), F32)],
        axis=0,
    )
    mine = (lanes((128, 128)) // 32 == rows((128, 128)) % 8) & (rows((128, 128)) < 24)
    head = jnp.where(mine, head, 0.0)
    fw_ref[...] = head[0:32].astype(BF16)
    fwt_ref[...] = jnp.transpose(head).astype(BF16)
    base[...] = jnp.zeros_like(base)
    base[0:1, 0:16] = b1_ref[...]
    base[1:2, 0:32] = b2_ref[...]
    base[8:14, 0:32] = wt_ref[...].astype(F32)
    pad = jnp.zeros((120, 128), F32)
    cols_ref[...] = jnp.transpose(jnp.concatenate([base[0:8, :], pad], axis=0))
    wtt_ref[0:32] = jnp.transpose(jnp.concatenate([base[8:16, :], pad], axis=0))[0:32]
    base[16:24, 0:6] = kt_ref[...].astype(F32)
    wtt_ref[32:40] = jnp.zeros((8, 128), F32)
    wtt_ref[32:33, 0:6] = bt_ref[...]
    place = place_ref[0]
    mine = rows((8, 128)) == place
    wtt_ref[33:34] = jnp.sum(jnp.where(mine, base[16:24], 0.0), axis=0, keepdims=True)
    dest = dest_ref[place]
    group = jnp.maximum(dest, 0) // 8
    live = jnp.where(dest >= 0, 1.0, 0.0)
    wtt_ref[34:35] = jnp.broadcast_to(live, (1, 128))
    wtt_ref[35:36] = jnp.broadcast_to(dest.astype(F32), (1, 128))
    for t in range(2):
        leads = side_of(lax.axis_index("yh") * 2 + t) == side_of(group % 4)
        here = jnp.where((dest >= 0) & leads, 1.0, 0.0)
        wtt_ref[36 + t : 37 + t] = jnp.broadcast_to(here, (1, 128))
    rank = jnp.float32(0)
    for e in range(8):
        other = dest_ref[e]
        twin = (other >= 0) & (jnp.maximum(other, 0) // 8 == group) & (e < place)
        rank = jnp.where(twin, 1.0, rank)
    wtt_ref[38:39] = jnp.broadcast_to(rank, (1, 128))
    row = rows((128, 1))
    bias = jnp.where(row < 8, bf_ref[0], jnp.where(row < 16, bf_ref[1], bf_ref[2]))
    cols_ref[:, 2:3] = bias


def step(
    flux_scale, tensor_scale, cell_count,
    got_ref,
    t1_ref, w2a_ref, wb_ref, wsb_ref, fw_ref, fwt_ref, cols_ref, wtt_ref, pick_ref,
    out_ref,
    a_ref, a2_ref, d_ref, dz1_ref, total, extra, sent,
):
    live = wtt_ref[34:35, 0:1]
    empty = jnp.zeros((8, 128), F32)

    def plane(z):
        if z < 0 or z > 15:
            return empty
        return got_ref[z // 2, z % 2].astype(F32)

    low = jnp.concatenate([plane(4 * q - 1 + zi) for zi in range(4) for q in range(4)], axis=0)
    high = jnp.concatenate([plane(4 * q + 1 + zi) for zi in range(4) for q in range(4)], axis=0)
    cells = jnp.concatenate([low, high], axis=1).astype(BF16)
    apart = mxu(cells, pick_ref[...])
    lines = []
    for zi in range(4):
        for xt in range(4):
            lines.append(
                jnp.concatenate(
                    [
                        apart[zi * 32 + q * 8 : zi * 32 + q * 8 + 8, xt * 128 : xt * 128 + 128]
                        for q in range(4)
                    ],
                    axis=1,
                )
            )
    lines.append(jnp.where(rows((16, CELLS)) == 0, 1.0, 0.0))
    xcol = jnp.concatenate(lines, axis=0).astype(BF16)
    b1 = jnp.concatenate([cols_ref[0:16, 0:1]] * 4, axis=0)
    zero = jnp.zeros((), BF16)
    first_z = lanes((16, CELLS)) < 64
    first_x = lanes((48, CELLS)) % 64 == 0
    a_ref[0:TALL] = jnp.zeros((TALL, CELLS), BF16)
    z1_all = mxu(t1_ref[...], xcol[0:128])
    for y in range(8):
        z1 = z1_all[y * 64 : y * 64 + 64] + b1
        act = jnp.maximum(z1, 0.0).astype(BF16)
        at = (y + 1) * TALL
        for px in range(2):
            moved = pltpu.roll(act[px * 32 + 16 : px * 32 + 32], 64, 1)
            moved = jnp.where(first_z, zero, moved)
            a_ref[at + px * 48 : at + px * 48 + 32] = act[px * 32 : px * 32 + 32]
            a_ref[at + px * 48 + 32 : at + px * 48 + 48] = moved
        a_ref[at + BLOCK : at + TALL] = act[0:16]
        late = jnp.concatenate([act[32:64], moved], axis=0)
        a_ref[at + 96 : at + BLOCK] = jnp.where(first_x, zero, pltpu.roll(late, 1, 1))
    b2 = cols_ref[0:32, 1:2]
    pooled = jnp.zeros((32, 1), F32)
    for y in range(4):
        at = 2 * y * TALL
        z2 = mxu(w2a_ref[:, 0:480], a_ref[at : at + 480]) + b2
        act = jnp.maximum(z2, 0.0).astype(BF16)
        a2_ref[y * 32 : y * 32 + 32] = act
        pooled = pooled + jnp.sum(act.astype(F32), axis=1, keepdims=True)
    pooled = pooled / cell_count
    a2 = a2_ref[...]
    head = wtt_ref[0:32]
    tensor = jnp.sum(head * pooled, axis=0, keepdims=True) + wtt_ref[32:33]
    dt = tensor_scale * (tensor - wtt_ref[33:34]) * live
    spread = jnp.sum(head * dt, axis=1, keepdims=True) / cell_count
    row = rows((24, 1))
    full = mxu(fw_ref[0:24], a2) + cols_ref[0:24, 2:3]
    goals = [
        jnp.concatenate(
            [
                got_ref[2 * q, 2 + h].astype(F32)
                + pltpu.roll(got_ref[2 * q + 1, 2 + h].astype(F32), 64, 1)
                for q in range(4)
            ],
            axis=1,
        )
        for h in range(2)
    ]
    wanted = jnp.concatenate([goals[0], pltpu.roll(goals[0], 4, 0), goals[1]], axis=0)
    diff = flux_scale * (full - wanted) * live
    df = jnp.where(row % 8 < 4, diff, 0.0)
    df = jnp.concatenate([df, jnp.zeros((8, CELLS), F32)], axis=0).astype(BF16)
    member = lanes((8, CELLS)) // 64 == rows((8, CELLS))
    shares = []
    for f in range(3):
        for y in range(4):
            line = jnp.where(member, full[f * 8 + y : f * 8 + y + 1], 0.0)
            line = (line[:, 0:128] + line[:, 128:256]) + (line[:, 256:384] + line[:, 384:512])
            shares.append(line + pltpu.roll(line, 64, 1))
    left = lanes((8, 128)) < 64
    lane8 = lanes((8, 128))
    dest = wtt_ref[35:36]
    slot = dest - 8.0 * jnp.floor(dest / 8.0) + 1.0
    last = jnp.where(lane8 < 6, jnp.broadcast_to(tensor, (8, 128)), 0.0)
    last = jnp.where(lane8 == 6, dest, last)
    last = jnp.where(lane8 == 7, wtt_ref[38:39], last)
    last = jnp.where(lane8 == 8, slot, last)
    for t in range(2):
        here = wtt_ref[36 + t : 37 + t] > 0
        for k in range(6):
            both = jnp.where(left, shares[2 * k], shares[2 * k + 1])
            sent[t * 8 : t * 8 + 8, 8 + k, :] = jnp.where(here, both, 0.0)
        sent[t * 8 : t * 8 + 8, 14, :] = jnp.where(
            here, last, jnp.where(lane8 == 6, -1.0, 0.0)
        )
        sent[t * 8 : t * 8 + 8, 15, :] = jnp.zeros((8, 128), F32)
    last_x = lanes((32, CELLS)) % 64 == 63
    last_z = lanes((32, CELLS)) >= 448
    bias2 = jnp.zeros((32, 1), F32)
    dz2 = []
    for y in range(4):
        da2 = mxu(fwt_ref[y * 32 : y * 32 + 32, 0:32], df) + spread
        d = jnp.where(a2_ref[y * 32 : y * 32 + 32] > 0, da2, 0.0).astype(BF16)
        wide = d.astype(F32)
        bias2 = bias2 + jnp.sum(wide, axis=1, keepdims=True)
        next_x = jnp.where(last_x, zero, pltpu.roll(d, CELLS - 1, 1))
        next_z = jnp.where(last_z, zero, pltpu.roll(d, CELLS - 64, 1))
        both = jnp.where(last_x | last_z, zero, pltpu.roll(d, CELLS - 65, 1))
        d_ref[y * 128 : y * 128 + 32] = d
        d_ref[y * 128 + 32 : y * 128 + 64] = next_x
        d_ref[y * 128 + 64 : y * 128 + 96] = next_z
        d_ref[y * 128 + 96 : y * 128 + 128] = both
        dz2.append(d)
    d_ref[512:640] = jnp.zeros((128, CELLS), BF16)
    none = jnp.zeros((32, CELLS), BF16)
    second = jnp.zeros((BLOCK, 128), F32)
    for y in range(4):
        at = (2 * y + 1) * TALL
        da1 = mxu(wb_ref[...], d_ref[y * 128 : y * 128 + 256])
        short = mxu(wsb_ref[:, 0:32], dz2[y])
        da1 = jnp.concatenate([da1[0:16] + short, da1[16:128]], axis=0)
        for sub in range(2):
            act = a_ref[at + sub * TALL : at + sub * TALL + BLOCK]
            if sub == 0:
                sides = [none, dz2[y], none, none]
            else:
                sides = [dz2[y + 1] if y < 3 else none, none, dz2[y], none]
            second = second + mxu(act, jnp.concatenate(sides, axis=0), NT)
            on = jnp.concatenate([act[0:32], act[48:80]], axis=0) > 0
            dz1 = jnp.where(on, da1[sub * 64 : sub * 64 + 64], 0.0).astype(BF16)
            dz1_ref[(2 * y + sub) * 64 : (2 * y + sub) * 64 + 64] = dz1
    parts = mxu(dz1_ref[...], xcol, NT)
    place8 = lanes((64, 128)) % 8
    fold = jnp.zeros((64, 128), F32)
    tail = jnp.zeros((64, 1), F32)
    for y in range(8):
        part = parts[y * 64 : y * 64 + 64, 0:128]
        tail = tail + parts[y * 64 : y * 64 + 64, 128:129]
        if y == 0:
            part = jnp.where(place8 == 7, 0.0, part)
        if y == 7:
            part = jnp.where(place8 == 0, 0.0, part)
        if y != 1:
            part = pltpu.roll(part, (1 - y) % 128, 1)
        fold = fold + part
    first = jnp.zeros((16, 128), F32)
    first_bias = jnp.zeros((16, 1), F32)
    for px in range(2):
        for z in range(2):
            at, left = px * 32 + z * 16, z * 32 + px * 8
            part = fold[at : at + 16]
            first = first + (pltpu.roll(part, 128 - left, 1) if left else part)
            first_bias = first_bias + tail[at : at + 16]
    lane = lanes((1, 128))
    bias2 = jnp.where(lanes((32, 128)) == 0, bias2, pooled * pltpu.roll(dt, 1, 1))
    upright = jnp.concatenate(
        [
            jnp.where(lanes((16, 128)) == 127, first_bias, first),
            jnp.zeros((16, 128), F32),
            bias2,
            jnp.zeros((64, 128), F32),
        ],
        axis=0,
    )
    upright = jnp.transpose(upright)
    cross = mxu(df, a2, NT)
    same = lanes((32, 128)) // 32 == rows((32, 128)) % 8
    cross = jnp.where(same, cross, 0.0)
    cross = cross + pltpu.roll(cross, 64, 1)
    cross = cross + pltpu.roll(cross, 32, 1)
    flux_sum = jnp.sum(df.astype(F32), axis=1, keepdims=True)
    for ky in range(3):
        tail_block = pltpu.roll(second[128:144], (96 - ky * 32) % 128, 1)
        extra[ky * 16 : ky * 16 + 16] = tail_block
    lane8, row8 = lanes((8, 128)), rows((8, 128))
    for i in range(5):
        pair = jnp.zeros((8, 128), F32)
        for h in range(2 if i < 4 else 1):
            g = 2 * i + h
            at = (g // 3) * 32 + (g % 3) * 8
            part = jnp.where(lane8 < 16, upright[at : at + 8], 0.0)
            pair = pair + pltpu.roll(part, 96 + 16 * h, 1)
        extra[48 + 3 * i : 51 + 3 * i] = pair[0:3]
    bias_row = jnp.zeros((1, 128), F32)
    for f in range(3):
        extra[63 + f : 64 + f] = jnp.sum(cross[f * 8 : f * 8 + 8], axis=0, keepdims=True)
        sums = jnp.sum(flux_sum[f * 8 : f * 8 + 8], axis=0, keepdims=True)
        bias_row = jnp.where(lane == 112 + f, sums, bias_row)
    extra[66:67] = pltpu.roll(upright[0:1], 64, 1)
    first_row = pltpu.roll(jnp.where(lane < 16, upright[127:128], 0.0), 96, 1)
    tensor_row = pltpu.roll(jnp.where(lane < 6, dt, 0.0), 116, 1)
    extra[67:68] = first_row + bias_row + tensor_row
    extra[68:74] = pltpu.roll(upright[0:8], 64, 1)[1:7]
    extra[74:80] = jnp.zeros((6, 128), F32)
    rest = lane8 >= 96
    remainder = ((row8 == 5) | (row8 == 6)) & rest
    swap = lax.axis_index("yh") * 8
    for t in range(16):
        block = second[t * 8 : t * 8 + 8]
        total[t * 8 : t * 8 + 8] = jnp.where(rest, 0.0, block)
        tail_rows = extra[t * 3 : t * 3 + 3]
        other_rows = extra[48 + t * 2 : 50 + t * 2]
        total[t * 8 : t * 8 + 3] = jnp.where(rest[0:3], tail_rows, block[0:3])
        total[t * 8 + 3 : t * 8 + 5] = jnp.where(rest[0:2], other_rows, block[3:5])
        block = total[t * 8 : t * 8 + 8]
        high = block.astype(BF16).astype(F32)
        to = lax.rem(t + swap, 16)
        sent[to, 0:8, :] = jnp.where(remainder, pltpu.roll(block - high, 2, 0), high)
    out_ref[...] = sent[...].astype(BF16)


def route(got_ref, out_ref, recs):
    recs[...] = got_ref[...].astype(F32)
    count = got_ref.shape[0]
    full = recs[0, 0:8, :]
    for p in range(1, count):
        full = full + recs[p, 0:8, :]
    row8, lane8 = rows((8, 128)), lanes((8, 128))
    split = ((row8 == 3) | (row8 == 4)) & (lane8 >= 96)
    full = full + jnp.where(split, pltpu.roll(full, 6, 0), 0.0)
    high = full.astype(BF16).astype(F32)
    low = full - high
    peers = out_ref.shape[0]
    lane = lanes((count, 128))
    last = recs[:, 14, :]
    dest = jnp.sum(jnp.where(lane == 6, last, 0.0), axis=1, keepdims=True).astype(jnp.int32)
    rank = jnp.sum(jnp.where(lane == 7, last, 0.0), axis=1, keepdims=True).astype(jnp.int32)
    side = side_of(lax.axis_index("yh") * 2 + lax.axis_index("yl"))
    peer = lane // 4
    group = (peer // 2) * 4 + jnp.where(peer % 2 == 0, side, 3 - side)
    seat = (rows((count, 128)) // 8) * 2 + rank
    right = (dest >= group * 8) & (dest < group * 8 + 8) & (seat == lane % 4)
    hit = jnp.where(right & (peer < peers), 1.0, 0.0)
    hit = jnp.concatenate([hit, jnp.zeros((128 - count, 128), F32)], axis=0)
    choose = jnp.transpose(hit)[0 : 4 * peers, 0:count].astype(BF16)
    layers = [mxu(choose, recs[:, 8 + k, :].astype(BF16)) for k in range(6)]
    marks = mxu(choose, last.astype(BF16))
    lane = lanes((4 * peers, 128))
    marks = jnp.where(lane == 6, pltpu.roll(marks, 126, 1), jnp.where(lane < 6, marks, 0.0))
    marks = [pltpu.roll(marks, 96 + 8 * j, 1) for j in range(4)]
    row8, lane8 = rows((8, 128)), lanes((8, 128))
    upper, spare = row8 < 4, (row8 == 7) & (lane8 >= 96)
    remainder = ((row8 == 5) | (row8 == 6)) & (lane8 >= 96)
    share = jnp.where(remainder, pltpu.roll(low, 2, 0), high)
    for i in range(peers):
        seats = marks[0][4 * i : 4 * i + 1]
        for j in range(1, 4):
            seats = seats + marks[j][4 * i + j : 4 * i + j + 1]
        tall = [jnp.where(spare, seats, share)]
        at = (i // 2) * 8
        for m in range(3):
            even, odd = layers[2 * m][at : at + 8], layers[2 * m + 1][at : at + 8]
            if i % 2 == 0:
                tall.append(jnp.where(upper, even, pltpu.roll(odd, 4, 0)))
            else:
                tall.append(jnp.where(upper, pltpu.roll(even, 4, 0), odd))
        out_ref[i] = jnp.concatenate(tall, axis=0).astype(BF16)


def spread(got_ref, out_ref):
    parts = jnp.sum(got_ref[:, 0:8, :].astype(F32), axis=0)
    row8 = rows((8, 128))
    split = ((row8 == 3) | (row8 == 4)) & (lanes((8, 128)) >= 96)
    share = parts + jnp.where(split, pltpu.roll(parts, 6, 0), 0.0)
    out_ref[...] = jnp.broadcast_to(share[None], out_ref.shape)


def pick_records(got_ref, recs):
    recs[...] = got_ref[...].astype(F32)
    count = got_ref.shape[0]
    marks = [pltpu.roll(recs[:, 7, :], 32 - 8 * j, 1) for j in range(4)]
    marks = jnp.concatenate(marks, axis=0)
    lane = lanes((4 * count, 128))
    slot = jnp.sum(jnp.where(lane == 6, marks, 0.0), axis=1, keepdims=True) - 1.0
    hit = jnp.where((slot == lane.astype(F32)) & (lane < 8), 1.0, 0.0)
    hit = hit.astype(BF16)
    held = [
        jnp.concatenate([recs[:, 8 + 4 * k + j, :] for j in range(4)], axis=0)
        for k in range(6)
    ]
    every = mxu(hit, jnp.concatenate(held + [marks], axis=1).astype(BF16), TN)[0:8]
    return every


def finish(
    got_ref, routed_ref,
    fp_ref, tp_ref, g1_ref, b1_ref, g2_ref, b2_ref, gs_ref, gf_ref, bf_ref, gt_ref, bt_ref,
    total, extra, second, recs,
):
    every = pick_records(routed_ref, recs)
    swap = lax.axis_index("yh") * 8
    for p in range(16):
        block = got_ref[lax.rem(p + swap, 16)]
        total[p * 8 : p * 8 + 8] = block
        extra[p * 3 : p * 3 + 3] = block[0:3, 96:128]
        extra[48 + p * 2 : 50 + p * 2] = block[3:5, 96:128]
    for kz in range(3):
        for ky in range(3):
            for kx in range(3):
                g = kz * 3 + kx
                at, to = 48 + 3 * (g // 2) + ky, 16 * (g % 2)
                g1_ref[(kz * 3 + ky) * 3 + kx] = extra[at : at + 1, to : to + 16]
    for ky in range(3):
        second[0:128] = total[0:128, ky * 32 : ky * 32 + 32]
        second[128:144] = extra[ky * 16 : ky * 16 + 16]
        for s, kx in enumerate((1, 2, 0)):
            for zo, kz in enumerate((1, 2, 0)):
                to = ((kz * 3 + ky) * 3 + kx) * 16
                part = second[s * 48 + zo * 16 : s * 48 + zo * 16 + 16]
                g2_ref[to : to + 16] = part
                if ky == 1 and kx == 1 and kz == 1:
                    gs_ref[...] = part
    gf_ref[...] = extra[63:66]
    b2_ref[...] = extra[66:67]
    b1_ref[...] = extra[67:68, 0:16]
    bf_ref[...] = extra[67:68, 16:19]
    bt_ref[...] = extra[67:68, 20:26]
    gt_ref[...] = extra[68:74]
    for k in range(6):
        got = every[:, k * 128 : k * 128 + 128].astype(BF16)
        f, y = (2 * k) // 4, (2 * k) % 4
        fp_ref[:, f, y, :] = got[:, 0:64]
        fp_ref[:, f, y + 1, :] = got[:, 64:128]
    tp_ref[...] = every[:, 768:774].astype(BF16)


SMEM = pl.BlockSpec(memory_space=pltpu.SMEM)
VMEM = pl.BlockSpec(memory_space=pltpu.VMEM)
MIB = 1024 * 1024


def run(kernel, name, scalars, arrays, outs, scratch=(), held=None, limit=16):
    return pl.pallas_call(
        kernel,
        out_shape=tuple(jax.ShapeDtypeStruct(*o[0:2]) for o in outs),
        in_specs=[SMEM] * len(scalars) + [held or VMEM] * len(arrays),
        out_specs=tuple(o[2] if len(o) > 2 else VMEM for o in outs),
        scratch_shapes=[pltpu.VMEM(*s) if isinstance(s, tuple) else s for s in scratch],
        compiler_params=pltpu.CompilerParams(vmem_limit_bytes=limit * MIB),
        name=name,
    )(*scalars, *arrays)


def exchange(block, axis, groups=None):
    return lax.all_to_all(block, axis, 0, 0, tiled=True, axis_index_groups=groups)


def on_device(
    volume, flux_target, tensor_target, dest,
    first_weight, first_bias, second_weight, second_bias, short_weight,
    flux_weight, flux_bias, tensor_weight, tensor_bias,
):
    depth, slabs = lax.axis_size("z"), lax.axis_size("slab")
    near, far = 2 * slabs, 2 * depth
    lines = [[z * 4 + y for z in range(depth) for y in pair] for pair in ((0, 3), (1, 2))]
    records = 8 * depth * 4
    flux_count = records * 3 * slabs * 4 * 64
    tensor_count = records * 6
    cell_count = slabs * 4 * 64
    place = lax.axis_index("slab").astype(jnp.int32).reshape(1)
    goal = jnp.pad(flux_target[:, :, 0], ((0, 0), (0, 1), (0, 0), (0, 64)))
    mine = jnp.concatenate([volume, goal.reshape(8, 2, 8, 128)], axis=1)
    record = exchange(mine, "slab")
    weights = run(
        prepare, "prepare", [place, dest, flux_bias],
        [
            jnp.transpose(first_weight[:, 0], (1, 2, 3, 0)),
            jnp.transpose(second_weight, (2, 3, 4, 1, 0)).reshape(432, 32),
            jnp.transpose(short_weight),
            flux_weight, tensor_weight,
            first_bias.reshape(1, 16), second_bias.reshape(1, 32), tensor_bias.reshape(1, 6),
            tensor_target,
        ],
        [
            ((512, 128), BF16), ((32, 512), BF16), ((128, 256), BF16), ((16, 128), BF16),
            ((32, 128), BF16), ((128, 128), BF16), ((128, 128), F32), ((40, 128), F32),
            ((256, CELLS), BF16),
        ],
        [((96, 128), F32), ((512, 128), F32)],
    )
    (terms,) = run(
        functools.partial(step, 2.0 / flux_count, 2.0 / tensor_count, float(cell_count)),
        "step", [], [record, *weights], [((near, SENT, 128), BF16)],
        [
            ((9 * TALL, CELLS), BF16), ((128, CELLS), BF16), ((640, CELLS), BF16),
            ((CELLS, CELLS), BF16), ((ROWS, 128), F32), ((112, 128), F32),
            ((near, SENT, 128), F32),
        ],
    )
    terms = exchange(terms, ("yl", "slab"))
    (routed,) = run(
        route, "route", [], [terms], [((far, ROUTED, 128), BF16)],
        [((near, SENT, 128), F32)],
    )
    routed = exchange(routed, ("z", "yh", "yl"), lines)
    (share,) = run(spread, "spread", [], [routed], [((near, 8, 128), F32)])
    total = exchange(share, ("yl", "slab"))
    fp, tp, g1, b1, g2, b2, gs, gf, bf, gt, bt = run(
        finish, "finish", [], [total, routed],
        [
            ((8, 3, 4, 64), BF16), ((8, 6), BF16),
            ((27, 1, 16), F32), ((1, 16), F32), ((432, 32), F32), ((1, 32), F32),
            ((16, 32), F32), ((3, 32), F32), ((1, 3), F32), ((6, 32), F32), ((1, 6), F32),
        ],
        [
            ((ROWS, 128), F32), ((112, 32), F32), ((BLOCK, 32), F32),
            ((far, ROUTED, 128), F32),
        ],
    )
    return (
        fp[:, :, None],
        tp,
        jnp.transpose(g1.reshape(3, 3, 3, 1, 16), (4, 3, 0, 1, 2)),
        b1.reshape(16),
        jnp.transpose(g2.reshape(3, 3, 3, 16, 32), (4, 3, 0, 1, 2)),
        b2.reshape(32),
        jnp.transpose(gs),
        gf,
        bf.reshape(3),
        gt,
        bt.reshape(6),
    )


def solution(mesh):
    grid = mesh.devices.reshape(-1, 2, 2, mesh.shape["slab"])
    mesh = jax.sharding.Mesh(grid, ("z", "yh", "yl", "slab"))
    groups = ("z", "yh", "yl")
    cells = P(groups, "slab", None, None)
    fields = P(groups, None, "slab", None, None)
    return jax.shard_map(
        on_device,
        mesh=mesh,
        in_specs=(cells, fields, P(groups, None), P(groups)) + (P(),) * 9,
        out_specs=(fields, P(groups, None)) + (P(),) * 9,
        check_vma=False,
    )
```
